128 devices in a mesh: radial: 16 (over x, y), col: 8 (over z, core).
Axes of the slice: x: 4, y: 4, z: 4, core: 2. Of those that a mesh axis runs over, the one named last changes fastest.
Arguments:
- forcing: bfloat16 [4, 32, 2, 128, 1024], P(None, 'radial', None, None, 'col'), may hold values from -6 to 6
- inverses: bfloat16 [4, 32, 2, 1024, 1024], P(None, 'radial', None, None, 'col'), may hold values from -0.125 to 0.125
- couplings: bfloat16 [4, 32, 2, 2, 1024, 1024], P(None, 'radial', None, None, None, 'col'), may hold values from -0.09375 to 0.09375
Outputs:
- solution: float32 [4, 32, 2, 128, 1024], P(None, 'radial', None, None, 'col')
The draws below stay inside these ranges and needn't reach their ends.
All inputs are finite; a program needn't handle non-finite values.
Results may differ from the reference program's by a relative error of at most 0.0085.
Values may be sent and summed in bfloat16 or wider, within the bound.
A program may use at most 128 MiB of HBM per device.

```python
import jax
import jax.numpy as jnp
from jax import lax

BLOCK = 1024
LEVELS = 5
RHS = 128
FREQS = 4
ROWS = 32


def levels(key, dims, cuts, low, largest):
    level = 1.0
    for dim, shards_of in cuts:
        heights = jax.random.uniform(jax.random.fold_in(jax.random.fold_in(key, 6), dim), (shards_of,), jnp.float32, low / len(cuts), largest / len(cuts))
        level = level * jnp.repeat(jnp.exp(heights), dims[dim] // shards_of).reshape((-1,) + (1,) * (len(dims) - 1 - dim))
    return level


def bell_draw(key, dims, spread, bound, pieces=(), kind=jnp.bfloat16):
    loudness = levels(key, dims, pieces, -0.22, 0.18) if pieces else 1.0
    values = jax.random.normal(key, dims, jnp.float32) * spread * loudness
    return jnp.minimum(jnp.maximum(values, -bound), bound).astype(kind)


def setup_inputs(seed: int = 0) -> dict:
    splits = jax.random.split(jax.random.key(seed), 4)
    return {
        "forcing": bell_draw(splits[0], (FREQS, ROWS, 2, RHS, BLOCK), 1.0, 6.0, ((1, 16), (4, 8))),
        "inverses": bell_draw(splits[1], (FREQS, ROWS, 2, BLOCK, BLOCK), (2 * BLOCK) ** -0.5, 0.125, ((1, 16), (4, 8))),
        "couplings": bell_draw(splits[2], (FREQS, ROWS, 2, 2, BLOCK, BLOCK), (4 * BLOCK) ** -0.5, 0.09375, ((1, 16), (5, 8))),
    }


def conj_product(panel, factor):
    rounded = lax.optimization_barrier(panel.astype(jnp.bfloat16)).astype(jnp.float32)
    factor = factor.astype(jnp.float32)
    high = lax.Precision.HIGHEST
    real_part = jnp.einsum("frk,fkn->frn", rounded[:, 0], factor[:, 0], precision=high)
    real_part = real_part + jnp.einsum("frk,fkn->frn", rounded[:, 1], factor[:, 1], precision=high)
    imag_part = jnp.einsum("frk,fkn->frn", rounded[:, 1], factor[:, 0], precision=high)
    imag_part = imag_part - jnp.einsum("frk,fkn->frn", rounded[:, 0], factor[:, 1], precision=high)
    return jnp.stack([real_part, imag_part], axis=1)


def reference(forcing, inverses, couplings):
    panels = [forcing[:, target].astype(jnp.float32) for target in range(ROWS)]
    for depth_level in range(LEVELS):
        stride = 2 ** depth_level
        for target in range(stride, ROWS, 2 * stride):
            panels[target - stride] = panels[target - stride] - conj_product(panels[target], couplings[:, target, 0])
    solved = [None] * ROWS
    solved[0] = conj_product(panels[0], inverses[:, 0])
    for depth_level in reversed(range(LEVELS)):
        stride = 2 ** depth_level
        for target in range(stride, ROWS, 2 * stride):
            result = conj_product(panels[target], inverses[:, target])
            solved[target] = result - conj_product(solved[target - stride], couplings[:, target, 1])
    return jnp.stack(solved, axis=1)
```

```python
import functools

import jax
import jax.numpy as jnp
from jax import lax
from jax.experimental import pallas as pl
from jax.experimental.pallas import tpu as pltpu
from jax.sharding import PartitionSpec as P

MESH = pl.DeviceIdType.MESH
BF16 = jnp.bfloat16
F32 = jnp.float32
CHIPS = 4
CUTS = 4
LAG = 3
C0_ODD, C0_EVEN, I_EVEN, I_ODD, C1_EVEN, C1_ODD = range(6)


def kernel(
    force, inverse, coupling, out,
    fac, odd_v, even_f, base, red, upd, upd_out, inv_even, inv_odd, low, own, stage, acc,
    fac_sem, odd_sem, even_sem, base_sem, upd_sem, low_sem, own_sem, out_sem,
    fac_sent, odd_sent, even_sent, base_sent, upd_sent, low_sent, own_sent, out_sent, out_kept,
):
    chunks = base.shape[0]
    rhs = force.shape[3]
    cut = rhs // CUTS
    half = rhs // 2
    p = lax.axis_index("radial")
    c = lax.axis_index("col")
    z = lax.div(c, 2)
    k = lax.rem(c, 2)
    other = 1 - k
    levels = 4
    height = jnp.where(
        lax.rem(p, 2) == 1, 0,
        jnp.where(lax.rem(p, 4) == 2, 1, jnp.where(lax.rem(p, 8) == 4, 2, jnp.where(p == 8, 3, 4))),
    )
    reach = jnp.where(height == 0, 1, jnp.where(height == 1, 2, jnp.where(height == 2, 4, 8)))
    top = p == 0
    below = jnp.where(top, 0, p - reach)

    def ring(step):
        return lax.rem(z + step, CHIPS)

    def remote(src, dst, sent, got, column, target):
        copy = pltpu.make_async_remote_copy(
            src_ref=src, dst_ref=dst, send_sem=sent, recv_sem=got,
            device_id=(column, target), device_id_type=MESH,
        )
        copy.start()

    def local(src, dst, sem):
        pltpu.make_async_copy(src, dst, sem).start()

    def await_bytes(ref, sem):
        pltpu.make_async_copy(ref, ref, sem).wait()

    def factor(which, freq):
        if which == I_EVEN or which == I_ODD:
            return inverse.at[freq, which - I_EVEN]
        row = {C0_ODD: 1, C0_EVEN: 0, C1_EVEN: 0, C1_ODD: 1}[which]
        return coupling.at[freq, row, 0 if which < I_EVEN else 1]

    for which in (C0_ODD, C0_EVEN, I_EVEN, I_ODD, C1_EVEN, C1_ODD):
        for g in range(2):
            local(factor(which, 2 * k + g), fac.at[which, g, k], fac_sem.at[which, g])
        if which == C0_ODD:
            local(force.at[pl.ds(2 * k, 2), 0], even_f.at[k], even_sem)
            for g in range(2):
                for h in range(2):
                    local(
                        force.at[2 * k + g, 1, :, pl.ds(h * half, half)],
                        odd_v.at[g, h, c], odd_sem.at[g, h],
                    )

    barrier = pltpu.get_barrier_semaphore()

    def greet(column, target):
        pl.semaphore_signal(barrier, inc=1, device_id=(column, target), device_id_type=MESH)

    for step in range(1, CHIPS):
        for core in range(2):
            greet(p, 2 * ring(step) + core)
    greet(p, 2 * z + other)

    @pl.when(p > 0)
    def _():
        for chip in range(CHIPS):
            greet(below, 2 * chip + k)

    for level in range(levels):
        @pl.when(level < height)
        def _():
            for chip in range(CHIPS):
                greet(p + 2**level, 2 * chip + k)

    pl.semaphore_wait(barrier, 7 + CHIPS * (height + jnp.where(top, 0, 1)))

    def lend(which):
        for g in range(2):
            remote(
                factor(which, 2 * other + g), fac.at[which, g, k], fac_sent, fac_sem.at[which, g],
                p, 2 * z + other,
            )

    lend(C0_ODD)
    remote(force.at[pl.ds(2 * other, 2), 0], even_f.at[k], even_sent, even_sem, p, 2 * z + other)
    for g in range(2):
        for h in range(2):
            for step in (1, 3, 2, 0):
                for core in range(2):
                    def send():
                        remote(
                            force.at[2 * core + g, 1, :, pl.ds(h * half, half)],
                            odd_v.at[g, h, c], odd_sent, odd_sem.at[g, h], p, 2 * ring(step) + core,
                        )
                    if step:
                        send()
                    else:
                        pl.when(core != k)(send)
    for which in (C0_EVEN, I_EVEN, I_ODD, C1_EVEN, C1_ODD):
        lend(which)

    def times(panel, which, g):
        wide = jnp.concatenate(
            [fac[which, g, 0, 0], fac[which, g, 1, 0], fac[which, g, 0, 1], fac[which, g, 1, 1]], axis=1
        )
        both = jnp.dot(panel, wide, preferred_element_type=F32)
        n = wide.shape[1] // 2
        real = both[:cut, :n] + both[cut:, n:]
        imag = both[cut:, :n] - both[:cut, n:]
        return jnp.concatenate([real, imag], axis=0)

    def across(ref, i):
        return jnp.concatenate([ref[i, chip] for chip in range(CHIPS)], axis=1)

    def place(i):
        g = lax.div(i, CUTS)
        q = lax.rem(i, CUTS)
        h = lax.div(q, CUTS // 2)
        r = lax.rem(q, CUTS // 2)
        return g, q, h, pl.multiple_of(r * cut, cut)

    def odd_panel(i):
        g, _, h, r = place(i)
        parts = [
            jnp.concatenate([odd_v[g, h, col, part, pl.ds(r, cut)] for col in range(2 * CHIPS)], axis=1)
            for part in range(2)
        ]
        return jnp.concatenate(parts, axis=0)

    def write_out(i, row, value):
        g, q, _, _ = place(i)
        at = pl.ds(pl.multiple_of(q * cut, cut), cut)
        for side in range(2):
            for part in range(2):
                stage[side, g, row, part, at] = value[part * cut:(part + 1) * cut, side * 128:(side + 1) * 128]
        local(stage.at[k, g, row, :, at], out.at[2 * k + g, row, :, at], out_kept)
        remote(
            stage.at[other, g, row, :, at], out.at[2 * k + g, row, :, at], out_sent, out_sem,
            p, 2 * z + other,
        )

    def reduce_odd(i):
        g, q, h, r = place(i)

        @pl.when(lax.rem(q, CUTS // 2) == 0)
        def _():
            await_bytes(odd_v.at[g, h], odd_sem.at[g, h])

        at = pl.ds(pl.multiple_of(q * cut, cut), cut)
        mine = jnp.concatenate(
            [
                jnp.concatenate([even_f[side, g, part, at] for side in range(2)], axis=1)
                for part in range(2)
            ],
            axis=0,
        )
        left = mine.astype(F32) - times(odd_panel(i), C0_ODD, g)
        base[i, z] = left.astype(BF16)
        for step in (1, 3, 2):
            remote(base.at[i, z], base.at[i, z], base_sent, base_sem.at[i], p, 2 * ring(step) + k)

    def solved(i, value):
        own[i, z] = value.astype(BF16)
        for level in range(levels):
            @pl.when(height == level + 1)
            def _():
                for chip in range(CHIPS):
                    remote(
                        own.at[i, z], low.at[i, z], low_sent.at[level], low_sem.at[i],
                        p + 2**level, 2 * chip + k,
                    )
        for step in (1, 3, 2):
            remote(own.at[i, z], own.at[i, z], own_sent, own_sem.at[i], p, 2 * ring(step) + k)
        write_out(i, 0, value)

    def reduce_even(i):
        g, _, _, _ = place(i)
        await_bytes(base.at[i, pl.ds(0, 3)], base_sem.at[i])

        @pl.when(height == 0)
        def _():
            red[i] = base[i]

        for level in range(levels):
            @pl.when(level < height)
            def _():
                await_bytes(upd.at[level, i], upd_sem.at[level, i])
                before = base[i].astype(F32) if level == 0 else acc[...]
                acc[...] = before - upd[level, i].astype(F32)

        @pl.when(height > 0)
        def _():
            red[i] = acc[...].astype(BF16)

        product = times(across(red, i), jnp.where(top, I_EVEN, C0_EVEN), g)

        @pl.when(p > 0)
        def _():
            upd_out[i] = product.astype(BF16)
            for chip in range(CHIPS):
                remote(
                    upd_out.at[i], upd.at[height, i, z], upd_sent, upd_sem.at[height, i],
                    below, 2 * chip + k,
                )

        @pl.when(top)
        def _():
            solved(i, product)

    def apply_inverses(i):
        g, _, _, _ = place(i)
        inv_odd[i] = times(odd_panel(i), I_ODD, g)

        @pl.when(p > 0)
        def _():
            inv_even[i] = times(across(red, i), I_EVEN, g)

    def back_even(i):
        g, _, _, _ = place(i)
        await_bytes(low.at[i], low_sem.at[i])
        solved(i, inv_even[i] - times(across(low, i), C1_EVEN, g))

    def back_odd(i):
        g, _, _, _ = place(i)
        await_bytes(own.at[i, pl.ds(0, 3)], own_sem.at[i])
        for level in reversed(range(levels - 1)):
            @pl.when(level + 1 < height)
            def _():
                remote(
                    own.at[i], low.at[i], low_sent.at[level], low_sem.at[i], p + 2**level, c
                )
        write_out(i, 1, inv_odd[i] - times(across(own, i), C1_ODD, g))

    leaf = height == 0
    at_even = jnp.where(leaf, LAG, chunks)
    at_inverse = jnp.where(leaf, LAG + chunks, chunks)
    at_back = jnp.where(leaf, LAG + chunks, chunks) + chunks
    at_odd = jnp.where(top, at_even, at_back) + LAG

    for g in range(2):
        await_bytes(fac.at[C0_ODD, g], fac_sem.at[C0_ODD, g])
    await_bytes(even_f, even_sem)

    def step(s, _):
        @pl.when(s < chunks)
        def _():
            reduce_odd(s)

        def during(start, work, needs=()):
            i = s - start

            @pl.when(jnp.logical_and(i >= 0, i < chunks))
            def _():
                for which, here in needs:
                    @pl.when(jnp.logical_and(i == 0, here))
                    def _():
                        for g in range(2):
                            await_bytes(fac.at[which, g], fac_sem.at[which, g])
                work(i)

        during(at_even, reduce_even, ((C0_EVEN, True), (I_EVEN, top)))
        during(
            at_inverse, apply_inverses,
            ((I_EVEN, p > 0), (I_ODD, True), (C1_EVEN, True), (C1_ODD, True)),
        )

        @pl.when(p > 0)
        def _():
            during(at_back, back_even)

        during(at_odd, back_odd)
        return 0

    lax.fori_loop(0, 3 * chunks + 2 * LAG, step, 0)

    await_bytes(fac.at[pl.ds(0, 3)], fac_sent)
    await_bytes(odd_v.at[:, :, pl.ds(0, 7)], odd_sent)
    await_bytes(even_f.at[0], even_sent)
    await_bytes(base.at[:, pl.ds(0, 3)], base_sent)
    await_bytes(own.at[:, pl.ds(0, 3)], own_sent)

    @pl.when(p > 0)
    def _():
        await_bytes(base, upd_sent)

    for level in range(levels):
        @pl.when(level < height)
        def _():
            await_bytes(low, low_sent.at[level])
    await_bytes(stage.at[0], out_kept)
    await_bytes(stage.at[0], out_sent)
    await_bytes(stage.at[0], out_sem)


def local_solve(force, inverse, coupling):
    freqs, _, _, rhs, cols = force.shape
    block = inverse.shape[3]
    chunks = 2 * CUTS
    rows = 2 * rhs // CUTS
    wide = 2 * cols
    dma = pltpu.SemaphoreType.DMA
    panel = (chunks, CHIPS, rows, wide)
    hbm = pl.BlockSpec(memory_space=pl.ANY)
    return pl.pallas_call(
        kernel,
        out_shape=jax.ShapeDtypeStruct(force.shape, F32),
        in_specs=[hbm] * 3,
        out_specs=hbm,
        scratch_shapes=[
            pltpu.VMEM((6, 2, 2, 2, block, cols), BF16),
            pltpu.VMEM((2, 2, 2 * CHIPS, 2, rhs // 2, cols), BF16),
            pltpu.VMEM((2, 2, 2, rhs, cols), BF16),
            pltpu.VMEM(panel, BF16),
            pltpu.VMEM(panel, BF16),
            pltpu.VMEM((4,) + panel, BF16),
            pltpu.VMEM((chunks, rows, wide), BF16),
            pltpu.VMEM((chunks, rows, wide), F32),
            pltpu.VMEM((chunks, rows, wide), F32),
            pltpu.VMEM(panel, BF16),
            pltpu.VMEM(panel, BF16),
            pltpu.VMEM((2, 2, 2, 2, rhs, cols), F32),
            pltpu.VMEM(panel[1:], F32),
            dma((6, 2)), dma((2, 2)), dma, dma((chunks,)), dma((4, chunks)), dma((chunks,)), dma((chunks,)), dma,
            dma, dma, dma, dma, dma, dma((4,)), dma, dma, dma,
        ],
        compiler_params=pltpu.CompilerParams(
            collective_id=0, has_side_effects=True, vmem_limit_bytes=48 * 2**20
        ),
        name="resolvent",
    )(force, inverse, coupling)


def solution(mesh):
    return jax.shard_map(
        local_solve,
        mesh=mesh,
        in_specs=(
            P(None, "radial", None, None, "col"),
            P(None, "radial", None, None, "col"),
            P(None, "radial", None, None, None, "col"),
        ),
        out_specs=P(None, "radial", None, None, "col"),
        check_vma=False,
    )
```

```python
import jax
import jax.numpy as jnp
from jax import lax
from jax.experimental import pallas as pl
from jax.experimental.pallas import tpu as pltpu
from jax.sharding import PartitionSpec as P

MESH = pl.DeviceIdType.MESH
BF16 = jnp.bfloat16
F32 = jnp.float32
CHIPS = 4
CUTS = 4
C0, INV, C1 = range(3)
MIDDLE = 3
SETTLE = 2


def kernel(
    force, inverse, coupling, out,
    fac, mid, upp, odd_v, even_f, base, shard, mid_out, up_base, up_mid, up_all, up_upd, up_out, up_red,
    up_inv, up_low, up_own, inv_even, inv_odd, low, own, stage, up_stage, acc,
    fac_sem, mid_sem, upp_sem, odd_sem, even_sem, base_sem, up_base_sem, up_mid_sem, up_all_sem, up_upd_sem,
    up_low_sem, up_own_sem, low_sem, own_sem, out_sem, out_core_sem, out_far_sem,
    fac_sent, mid_sent, upp_lent, upp_sent, odd_sent, even_sent, base_sent, shard_sent, mid_out_sent,
    up_all_sent, up_out_sent, up_first_sent, up_own_sent, full_sent, own_sent, out_sent, out_kept,
    up_stage_sent, up_stage_kept,
):
    chunks = base.shape[0]
    rhs = force.shape[3]
    cut = rhs // CUTS
    half = rhs // 2
    p = lax.axis_index("radial")
    c = lax.axis_index("col")
    x, y = lax.div(p, 4), lax.rem(p, 4)
    z, k = lax.div(c, 2), lax.rem(c, 2)
    other = 1 - k
    odd = lax.rem(y, 2) == 1
    even = lax.rem(y, 2) == 0
    kind_a = jnp.logical_or(y == 0, jnp.logical_and(odd, y == 1 + 2 * k))
    kind_b = jnp.logical_not(kind_a)
    up_g = lax.rem(y, 2)
    home = 4 * x + jnp.where(kind_a, 0, 2)
    height = jnp.where(kind_b, 0, jnp.where(lax.rem(x, 2) == 1, 1, jnp.where(x == 2, 2, 3)))
    top = height == 3
    inner = height < 3
    twin = 4 * x + lax.rem(y + 2, 4)
    parent = jnp.where(kind_b, twin, jnp.where(height == 1, p - 4, jnp.where(height == 2, p - 8, p)))
    first = jnp.where(height == 3, p + 8, jnp.where(height == 2, p + 4, twin))
    beside = 4 * x + lax.rem(y + 1 + 2 * k, 4)
    child = 4 * x + jnp.where(kind_a, 1, 3)
    child_here = child == p

    def both(one, two):
        return jnp.logical_and(one, two)

    def ring(step):
        return lax.rem(z + step, CHIPS)

    def remote(src, dst, sent, got, column, target):
        pltpu.make_async_remote_copy(
            src_ref=src, dst_ref=dst, send_sem=sent, recv_sem=got,
            device_id=(column, target), device_id_type=MESH,
        ).start()

    def local(src, dst, sem):
        pltpu.make_async_copy(src, dst, sem).start()

    def await_bytes(ref, sem):
        pltpu.make_async_copy(ref, ref, sem).wait()

    def factor(which, row, freq):
        if which == INV:
            return inverse.at[freq, row]
        return coupling.at[freq, row, 0 if which == C0 else 1]

    def keep(which, row, ref, sem):
        for g in range(2):
            local(factor(which, row, 2 * k + g), ref.at[which, g, k], sem.at[which, g])

    def lend(which, row, ref, sem, sent):
        for g in range(2):
            remote(
                factor(which, row, 2 * other + g), ref.at[which, g, k], sent, sem.at[which, g],
                p, 2 * z + other,
            )

    keep(C0, 1, fac, fac_sem)
    local(force.at[pl.ds(2 * k, 2), 0], even_f.at[k], even_sem)
    for g in range(2):
        for h in range(2):
            local(
                force.at[2 * k + g, 1, :, pl.ds(h * half, half)], odd_v.at[g, h, c], odd_sem.at[g, h]
            )
    for which in (C0, INV, C1):
        @pl.when(odd)
        def _():
            keep(which, 0, mid, mid_sem)

        @pl.when(even)
        def _():
            local(factor(which, 0, 2 * k), upp.at[which, k], upp_sem.at[which])

        if which != C0:
            keep(which, 1, fac, fac_sem)

    barrier = pltpu.get_barrier_semaphore()

    def greet(column, target):
        pl.semaphore_signal(barrier, inc=1, device_id=(column, target), device_id_type=MESH)

    for step in range(1, CHIPS):
        for core in range(2):
            greet(p, 2 * ring(step) + core)
    greet(p, 2 * z + other)
    for core in range(2):
        greet(4 * x + lax.rem(y + 1, 4), 2 * z + core)
        greet(4 * x + lax.rem(y + 3, 4), 2 * z + core)
    for chip in range(CHIPS):
        greet(twin, 2 * chip + k)

    @pl.when(y >= 2)
    def _():
        for step in range(1, CHIPS):
            greet(4 * x + 5 - y, 2 * ring(step) + k)

    def greet_chips(column):
        for chip in range(CHIPS):
            greet(column, 2 * chip + k)

    a_even = both(kind_a, lax.rem(x, 2) == 0)

    @pl.when(both(kind_a, height < 3))
    def _():
        greet_chips(parent)

    @pl.when(a_even)
    def _():
        greet_chips(p + 4)

    @pl.when(top)
    def _():
        greet_chips(p + 8)

    pl.semaphore_wait(
        barrier,
        15 + jnp.where(y >= 2, 3, 0) + jnp.where(kind_a, jnp.where(lax.rem(x, 2) == 0, 8, 4), 0),
    )

    lend(C0, 1, fac, fac_sem, fac_sent)
    remote(force.at[pl.ds(2 * other, 2), 0], even_f.at[k], even_sent, even_sem, p, 2 * z + other)
    for g in range(2):
        for h in range(2):
            for step in (1, 3, 2, 0):
                for core in range(2):
                    def send():
                        remote(
                            force.at[2 * core + g, 1, :, pl.ds(h * half, half)],
                            odd_v.at[g, h, c], odd_sent, odd_sem.at[g, h], p, 2 * ring(step) + core,
                        )
                    if step:
                        send()
                    else:
                        pl.when(core != k)(send)
    for which in (C0, INV, C1):
        @pl.when(odd)
        def _():
            lend(which, 0, mid, mid_sem, mid_sent)

        @pl.when(even)
        def _():
            for core in range(2):
                remote(
                    factor(which, 0, 2 * core + 1), upp.at[which, k], upp_sent, upp_sem.at[which],
                    4 * x + lax.rem(y + 1 + 2 * core, 4), 2 * z + core,
                )
            remote(
                factor(which, 0, 2 * other), upp.at[which, k], upp_lent, upp_sem.at[which],
                p, 2 * z + other,
            )

        if which != C0:
            lend(which, 1, fac, fac_sem, fac_sent)

    def times(panel, ref):
        wide = jnp.concatenate([ref[0, 0], ref[1, 0], ref[0, 1], ref[1, 1]], axis=1)
        product = jnp.dot(panel, wide, preferred_element_type=F32)
        n = wide.shape[1] // 2
        real = product[:cut, :n] + product[cut:, n:]
        imag = product[cut:, :n] - product[:cut, n:]
        return jnp.concatenate([real, imag], axis=0)

    def across(ref, i):
        return jnp.concatenate([ref[i, chip] for chip in range(CHIPS)], axis=1)

    def place(i):
        g = lax.div(i, CUTS)
        q = lax.rem(i, CUTS)
        h = lax.div(q, CUTS // 2)
        r = lax.rem(q, CUTS // 2)
        return g, q, h, pl.multiple_of(r * cut, cut)

    def rows_of(q):
        return pl.ds(pl.multiple_of(q * cut, cut), cut)

    def odd_panel(i):
        g, _, h, r = place(i)
        parts = [
            jnp.concatenate([odd_v[g, h, col, part, pl.ds(r, cut)] for col in range(2 * CHIPS)], axis=1)
            for part in range(2)
        ]
        return jnp.concatenate(parts, axis=0)

    def along(ref, i, sent, sem):
        for step in (1, 3, 2):
            remote(ref.at[i, z], ref.at[i, z], sent, sem.at[i], p, 2 * ring(step) + k)

    def straight(src, dst, sent, got, column):
        for chip in range(CHIPS):
            remote(src, dst, sent, got, column, 2 * chip + k)

    def write_out(i, row, value):
        g, q, _, _ = place(i)
        at = rows_of(q)
        for side in range(2):
            for part in range(2):
                stage[side, g, row, part, at] = value[part * cut:(part + 1) * cut, side * 128:(side + 1) * 128]
        local(stage.at[k, g, row, :, at], out.at[2 * k + g, row, :, at], out_kept)
        remote(
            stage.at[other, g, row, :, at], out.at[2 * k + g, row, :, at], out_sent, out_sem,
            p, 2 * z + other,
        )

    def write_upper(j, value):
        at = rows_of(j)
        freq = 2 * k + up_g
        for side in range(2):
            for part in range(2):
                up_stage[side, part, at] = value[part * cut:(part + 1) * cut, side * 128:(side + 1) * 128]

        @pl.when(even)
        def _():
            local(up_stage.at[k, :, at], out.at[freq, 0, :, at], up_stage_kept)
            remote(
                up_stage.at[other, :, at], out.at[freq, 0, :, at], up_stage_sent, out_core_sem,
                p, 2 * z + other,
            )

        @pl.when(odd)
        def _():
            for side in range(2):
                remote(
                    up_stage.at[side, :, at], out.at[freq, 0, :, at], up_stage_sent, out_far_sem,
                    home, 2 * z + side,
                )

    def await_factor(ref, which, sem):
        for g in range(2):
            await_bytes(ref.at[which, g], sem.at[which, g])

    def await_upper(which):
        await_bytes(upp.at[which], upp_sem.at[which])

    def once(i, work):
        pl.when(i == 0)(work)

    def reduce_odd(i):
        g, q, h, _ = place(i)

        @pl.when(lax.rem(q, CUTS // 2) == 0)
        def _():
            await_bytes(odd_v.at[g, h], odd_sem.at[g, h])

        at = rows_of(q)
        mine = jnp.concatenate(
            [
                jnp.concatenate([even_f[side, g, part, at] for side in range(2)], axis=1)
                for part in range(2)
            ],
            axis=0,
        )
        left = (mine.astype(F32) - times(odd_panel(i), fac.at[C0, g])).astype(BF16)

        @pl.when(odd)
        def _():
            base[i, z] = left
            along(base, i, base_sent, base_sem)

        @pl.when(both(even, g == 0))
        def _():
            up_base[q] = left

        @pl.when(both(even, g == 1))
        def _():
            shard[q] = left
            remote(shard.at[q], up_base.at[q], shard_sent, up_base_sem.at[q], beside, c)

    def reduce_middle(i):
        g, q, _, _ = place(i)
        once(i, lambda: await_factor(mid, C0, mid_sem))
        await_bytes(base.at[i, pl.ds(0, 3)], base_sem.at[i])
        mid_out[i] = times(across(base, i), mid.at[C0, g]).astype(BF16)

        @pl.when(g == 0)
        def _():
            remote(mid_out.at[i], up_mid.at[q], mid_out_sent, up_mid_sem.at[q], p - 1, c)

        @pl.when(both(g == 1, k == 0))
        def _():
            local(mid_out.at[i], up_mid.at[q], up_mid_sem.at[q])

        @pl.when(both(g == 1, k == 1))
        def _():
            remote(mid_out.at[i], up_mid.at[q], mid_out_sent, up_mid_sem.at[q], twin, c)

    def inverse_odd(i):
        g, _, _, _ = place(i)
        once(i, lambda: await_factor(fac, INV, fac_sem))
        inv_odd[i] = times(odd_panel(i), fac.at[INV, g])

    def inverse_middle(i):
        g, _, _, _ = place(i)
        once(i, lambda: await_factor(mid, INV, mid_sem))
        inv_even[i] = times(across(base, i), mid.at[INV, g])

    def settle_upper(j):
        @pl.when(odd)
        def _():
            await_bytes(up_base.at[j], up_base_sem.at[j])

        await_bytes(up_mid.at[j], up_mid_sem.at[j])
        up_all[j, z] = (up_base[j].astype(F32) - up_mid[j].astype(F32)).astype(BF16)
        along(up_all, j, up_all_sent, up_all_sem)

    def reduce_upper(j):
        @pl.when(j == 0)
        def _():
            await_upper(C0)

            @pl.when(top)
            def _():
                await_upper(INV)
                await_upper(C1)

        await_bytes(up_all.at[j, pl.ds(0, 3)], up_all_sem.at[j])

        @pl.when(height == 0)
        def _():
            up_red[j] = up_all[j]

        for level in range(3):
            @pl.when(level < height)
            def _():
                await_bytes(up_upd.at[level, j], up_upd_sem.at[level, j])
                before = up_all[j].astype(F32) if level == 0 else acc[...]
                acc[...] = before - up_upd[level, j].astype(F32)

        @pl.when(height > 0)
        def _():
            up_red[j] = acc[...].astype(BF16)

        product = times(across(up_red, j), upp.at[jnp.where(top, INV, C0)])

        @pl.when(inner)
        def _():
            up_out[j] = product.astype(BF16)
            straight(up_out.at[j], up_upd.at[height, j, z], up_out_sent, up_upd_sem.at[height, j], parent)

        @pl.when(top)
        def _():
            solved_upper(j, product)

    def inverse_upper(j):
        once(j, lambda: await_upper(INV))
        up_inv[j] = times(across(up_red, j), upp.at[INV])

    def solved_upper(j, value):
        up_own[j, z] = value.astype(BF16)

        @pl.when(height > 0)
        def _():
            straight(up_own.at[j, z], up_low.at[j, z], up_first_sent, up_low_sem.at[j], first)

        @pl.when(both(kind_b, jnp.logical_not(child_here)))
        def _():
            i = up_g * CUTS + j
            straight(up_own.at[j, z], low.at[i, z], up_first_sent, low_sem.at[i], child)

        along(up_own, j, up_own_sent, up_own_sem)
        write_upper(j, value)

    def pass_upper(j):
        i = up_g * CUTS + j
        await_bytes(up_own.at[j, pl.ds(0, 3)], up_own_sem.at[j])

        @pl.when(child_here)
        def _():
            local(up_own.at[j], low.at[i], low_sem.at[i])

        @pl.when(top)
        def _():
            remote(up_own.at[j], up_low.at[j], full_sent.at[0], up_low_sem.at[j], p + 4, c)

        @pl.when(a_even)
        def _():
            remote(up_own.at[j], up_low.at[j], full_sent.at[1], up_low_sem.at[j], twin, c)

        @pl.when(both(kind_a, jnp.logical_not(child_here)))
        def _():
            remote(up_own.at[j], low.at[i], full_sent.at[2], low_sem.at[i], child, c)

        @pl.when(odd)
        def _():
            remote(up_own.at[j], own.at[i], full_sent.at[3], own_sem.at[i], home, c)

    def back_upper(j):
        once(j, lambda: await_upper(C1))
        await_bytes(up_low.at[j], up_low_sem.at[j])
        solved_upper(j, up_inv[j] - times(across(up_low, j), upp.at[C1]))

    def back_middle(i):
        g, _, _, _ = place(i)
        once(i, lambda: await_factor(mid, C1, mid_sem))
        await_bytes(low.at[i], low_sem.at[i])
        value = inv_even[i] - times(across(low, i), mid.at[C1, g])
        own[i, z] = value.astype(BF16)
        along(own, i, own_sent, own_sem)
        write_out(i, 0, value)

    def back_odd(i):
        g, q, _, _ = place(i)
        once(i, lambda: await_factor(fac, C1, fac_sem))

        @pl.when(odd)
        def _():
            await_bytes(own.at[i, pl.ds(0, 3)], own_sem.at[i])

        @pl.when(both(even, g == 0))
        def _():
            own[i] = up_own[q]

        @pl.when(both(even, g == 1))
        def _():
            await_bytes(own.at[i], own_sem.at[i])

        write_out(i, 1, inv_odd[i] - times(across(own, i), fac.at[C1, g]))

    at_settle = jnp.where(even, MIDDLE + 3, MIDDLE + 7)
    at_upper = at_settle + jnp.where(kind_b, SETTLE, CUTS)
    at_middle_inverse = MIDDLE + 7 + 2 * CUTS
    at_back = at_middle_inverse + chunks
    at_pass = jnp.where(top, at_upper, at_back) + SETTLE
    at_end = at_back + 3

    for g in range(2):
        await_bytes(fac.at[C0, g], fac_sem.at[C0, g])
    await_bytes(even_f, even_sem)

    def step(s, _):
        def during(start, count, work, who=None):
            i = s - start
            now = both(i >= 0, i < count)

            @pl.when(now if who is None else both(now, who))
            def _():
                work(i)

        during(0, chunks, reduce_odd)
        during(MIDDLE, chunks, reduce_middle, odd)
        during(MIDDLE + 1, chunks, inverse_odd)
        during(at_settle, CUTS, settle_upper)
        during(at_upper, CUTS, reduce_upper)
        during(at_upper, CUTS, inverse_upper, inner)
        during(at_middle_inverse, chunks, inverse_middle, odd)
        during(at_back, CUTS, back_upper, inner)
        during(at_pass, CUTS, pass_upper)
        during(at_back, chunks, back_middle, odd)
        during(at_end, chunks, back_odd)
        return 0

    lax.fori_loop(0, MIDDLE + 7 + 2 * CUTS + chunks + 3 + chunks, step, 0)

    await_bytes(fac.at[:, 0], fac_sent)
    await_bytes(odd_v.at[:, :, pl.ds(0, 7)], odd_sent)
    await_bytes(even_f.at[0], even_sent)
    await_bytes(up_all.at[:, pl.ds(0, 3)], up_all_sent)
    await_bytes(up_own.at[:, pl.ds(0, 3)], up_own_sent)

    @pl.when(inner)
    def _():
        await_bytes(up_all, up_out_sent)

    @pl.when(jnp.logical_not(both(kind_b, child_here)))
    def _():
        await_bytes(up_all, up_first_sent)

    @pl.when(top)
    def _():
        await_bytes(up_all, full_sent.at[0])

    @pl.when(a_even)
    def _():
        await_bytes(up_all, full_sent.at[1])

    @pl.when(both(kind_a, jnp.logical_not(child_here)))
    def _():
        await_bytes(up_all, full_sent.at[2])

    @pl.when(odd)
    def _():
        await_bytes(mid.at[:, 0], mid_sent)
        await_bytes(base.at[:, pl.ds(0, 3)], base_sent)
        await_bytes(up_all, full_sent.at[3])
        await_bytes(own.at[:, pl.ds(0, 3)], own_sent)
        await_bytes(stage.at[0], out_kept)
        await_bytes(stage.at[0], out_sent)
        await_bytes(stage.at[0], out_sem)
        await_bytes(up_stage, up_stage_sent)

    @pl.when(both(odd, k == 0))
    def _():
        await_bytes(mid_out.at[pl.ds(0, CUTS)], mid_out_sent)

    @pl.when(both(odd, k == 1))
    def _():
        await_bytes(mid_out, mid_out_sent)

    @pl.when(even)
    def _():
        await_bytes(upp, upp_sent)
        await_bytes(upp.at[:, 0], upp_lent)
        await_bytes(shard, shard_sent)
        await_bytes(stage.at[0, 0], out_kept)
        await_bytes(stage.at[0, 0], out_sent)
        await_bytes(stage.at[0, 0], out_sem)
        await_bytes(up_stage.at[0], up_stage_kept)
        await_bytes(up_stage.at[0], up_stage_sent)
        await_bytes(up_stage.at[0], out_core_sem)
        await_bytes(up_stage, out_far_sem)


def local_solve(force, inverse, coupling):
    rhs, cols = force.shape[3:]
    block = inverse.shape[3]
    chunks = 2 * CUTS
    rows = 2 * rhs // CUTS
    wide = 2 * cols
    dma = pltpu.SemaphoreType.DMA
    piece = (rows, wide)
    panel = (chunks, CHIPS) + piece
    upper = (CUTS, CHIPS) + piece
    weight = (2, 2, block, cols)
    hbm = pl.BlockSpec(memory_space=pl.ANY)
    return pl.pallas_call(
        kernel,
        out_shape=jax.ShapeDtypeStruct(force.shape, F32),
        in_specs=[hbm] * 3,
        out_specs=hbm,
        scratch_shapes=[
            pltpu.VMEM((3, 2) + weight, BF16),
            pltpu.VMEM((3, 2) + weight, BF16),
            pltpu.VMEM((3,) + weight, BF16),
            pltpu.VMEM((2, 2, 2 * CHIPS, 2, rhs // 2, cols), BF16),
            pltpu.VMEM((2, 2, 2, rhs, cols), BF16),
            pltpu.VMEM(panel, BF16),
            pltpu.VMEM((CUTS,) + piece, BF16),
            pltpu.VMEM((chunks,) + piece, BF16),
            pltpu.VMEM((CUTS,) + piece, BF16),
            pltpu.VMEM((CUTS,) + piece, BF16),
            pltpu.VMEM(upper, BF16),
            pltpu.VMEM((3,) + upper, BF16),
            pltpu.VMEM((CUTS,) + piece, BF16),
            pltpu.VMEM(upper, BF16),
            pltpu.VMEM((CUTS,) + piece, F32),
            pltpu.VMEM(upper, BF16),
            pltpu.VMEM(upper, BF16),
            pltpu.VMEM((chunks,) + piece, F32),
            pltpu.VMEM((chunks,) + piece, F32),
            pltpu.VMEM(panel, BF16),
            pltpu.VMEM(panel, BF16),
            pltpu.VMEM((2, 2, 2, 2, rhs, cols), F32),
            pltpu.VMEM((2, 2, rhs, cols), F32),
            pltpu.VMEM((CHIPS,) + piece, F32),
            dma((3, 2)), dma((3, 2)), dma((3,)), dma((2, 2)), dma, dma((chunks,)), dma((CUTS,)), dma((CUTS,)),
            dma((CUTS,)), dma((3, CUTS)), dma((CUTS,)), dma((CUTS,)), dma((chunks,)), dma((chunks,)),
            dma, dma, dma,
            dma, dma, dma, dma, dma, dma, dma, dma, dma, dma, dma, dma, dma, dma((4,)), dma, dma, dma, dma, dma,
        ],
        compiler_params=pltpu.CompilerParams(
            collective_id=0, has_side_effects=True, vmem_limit_bytes=60 * 2**20
        ),
        name="resolvent",
    )(force, inverse, coupling)


def solution(mesh):
    return jax.shard_map(
        local_solve,
        mesh=mesh,
        in_specs=(
            P(None, "radial", None, None, "col"),
            P(None, "radial", None, None, "col"),
            P(None, "radial", None, None, None, "col"),
        ),
        out_specs=P(None, "radial", None, None, "col"),
        check_vma=False,
    )
```

```python
import jax
import jax.numpy as jnp
from jax import lax
from jax.experimental import pallas as pl
from jax.experimental.pallas import tpu as pltpu
from jax.sharding import PartitionSpec as P

MESH = pl.DeviceIdType.MESH
BF16 = jnp.bfloat16
F32 = jnp.float32
CHIPS = 4
CUTS = 4
C0, INV, C1 = range(3)
MIDDLE = 3
SETTLE = 2
PIECES = 8


def kernel(
    force, inverse, coupling, out,
    fac, mid, upp, odd_v, even_f, base, shard, mid_out, up_base, up_mid, up_all, up_upd, up_out, up_red,
    up_inv, up_low, up_own, inv_even, inv_odd, low, own, stage, up_stage, acc,
    fac_sem, mid_sem, upp_sem, odd_sem, even_sem, base_sem, up_base_sem, up_mid_sem, up_all_sem, up_upd_sem,
    up_low_sem, low_sem, own_sem, up_shard_sem, low_shard_sem, own_shard_sem, out_sem, out_core_sem, out_far_sem,
    fac_sent, mid_sent, upp_lent, upp_sent, odd_sent, even_sent, base_sent, shard_sent, mid_out_sent,
    up_all_sent, up_out_sent, up_first_sent, shard_out_sent, up_low_sent, low_sent, own_sent, out_sent, out_kept,
    up_stage_sent, up_stage_kept,
):
    chunks = base.shape[0]
    rhs = force.shape[3]
    cut = rhs // CUTS
    half = rhs // 2
    p = lax.axis_index("radial")
    c = lax.axis_index("col")
    x, y = lax.div(p, 4), lax.rem(p, 4)
    z, k = lax.div(c, 2), lax.rem(c, 2)
    other = 1 - k
    odd = lax.rem(y, 2) == 1
    even = lax.rem(y, 2) == 0
    kind_a = jnp.logical_or(y == 0, jnp.logical_and(odd, y == 1 + 2 * k))
    kind_b = jnp.logical_not(kind_a)
    up_g = lax.rem(y, 2)
    home = 4 * x + jnp.where(kind_a, 0, 2)
    height = jnp.where(kind_b, 0, jnp.where(lax.rem(x, 2) == 1, 1, jnp.where(x == 2, 2, 3)))
    top = height == 3
    inner = height < 3
    twin = 4 * x + lax.rem(y + 2, 4)
    parent = jnp.where(kind_b, twin, jnp.where(height == 1, p - 4, jnp.where(height == 2, p - 8, p)))
    first = jnp.where(height == 3, p + 8, jnp.where(height == 2, p + 4, twin))
    beside = 4 * x + lax.rem(y + 1 + 2 * k, 4)
    child = 4 * x + jnp.where(kind_a, 1, 3)
    child_here = child == p
    by_shard = jnp.logical_or(jnp.logical_and(height == 1, x == 1), jnp.logical_and(kind_b, lax.rem(x, 2) == 0))

    def both(one, two):
        return jnp.logical_and(one, two)

    def ring(step):
        return lax.rem(z + step, CHIPS)

    def remote(src, dst, sent, got, column, target):
        pltpu.make_async_remote_copy(
            src_ref=src, dst_ref=dst, send_sem=sent, recv_sem=got,
            device_id=(column, target), device_id_type=MESH,
        ).start()

    def local(src, dst, sem):
        pltpu.make_async_copy(src, dst, sem).start()

    def await_bytes(ref, sem):
        pltpu.make_async_copy(ref, ref, sem).wait()

    def factor(which, row, freq):
        if which == INV:
            return inverse.at[freq, row]
        return coupling.at[freq, row, 0 if which == C0 else 1]

    def keep(which, row, ref, sem):
        for g in range(2):
            local(factor(which, row, 2 * k + g), ref.at[which, g, k], sem.at[which, g])

    def lend(which, row, ref, sem, sent):
        for g in range(2):
            remote(
                factor(which, row, 2 * other + g), ref.at[which, g, k], sent, sem.at[which, g],
                p, 2 * z + other,
            )

    keep(C0, 1, fac, fac_sem)
    local(force.at[pl.ds(2 * k, 2), 0], even_f.at[k], even_sem)
    for g in range(2):
        for h in range(2):
            local(
                force.at[2 * k + g, 1, :, pl.ds(h * half, half)], odd_v.at[g, h, c], odd_sem.at[g, h]
            )
    for which in (C0, INV, C1):
        @pl.when(odd)
        def _():
            keep(which, 0, mid, mid_sem)

        @pl.when(even if which == INV else both(even, p > 0))
        def _():
            local(factor(which, 0, 2 * k), upp.at[which, k], upp_sem.at[which])

        if which != C0:
            keep(which, 1, fac, fac_sem)

    barrier = pltpu.get_barrier_semaphore()

    def greet(column, target):
        pl.semaphore_signal(barrier, inc=1, device_id=(column, target), device_id_type=MESH)

    for step in range(1, CHIPS):
        for core in range(2):
            greet(p, 2 * ring(step) + core)
    greet(p, 2 * z + other)
    for core in range(2):
        greet(4 * x + lax.rem(y + 1, 4), 2 * z + core)
        greet(4 * x + lax.rem(y + 3, 4), 2 * z + core)
    for chip in range(CHIPS):
        greet(twin, 2 * chip + k)

    @pl.when(y >= 2)
    def _():
        for step in range(1, CHIPS):
            greet(4 * x + 5 - y, 2 * ring(step) + k)

    def greet_chips(column):
        for chip in range(CHIPS):
            greet(column, 2 * chip + k)

    a_even = both(kind_a, lax.rem(x, 2) == 0)

    @pl.when(both(kind_a, height < 3))
    def _():
        greet_chips(parent)

    @pl.when(a_even)
    def _():
        greet_chips(p + 4)

    @pl.when(top)
    def _():
        greet_chips(p + 8)

    pl.semaphore_wait(
        barrier,
        15 + jnp.where(y >= 2, 3, 0) + jnp.where(kind_a, jnp.where(lax.rem(x, 2) == 0, 8, 4), 0),
    )

    lend(C0, 1, fac, fac_sem, fac_sent)
    remote(force.at[pl.ds(2 * other, 2), 0], even_f.at[k], even_sent, even_sem, p, 2 * z + other)
    for g in range(2):
        for h in range(2):
            for step in (1, 3, 2, 0):
                for core in range(2):
                    def send():
                        remote(
                            force.at[2 * core + g, 1, :, pl.ds(h * half, half)],
                            odd_v.at[g, h, c], odd_sent, odd_sem.at[g, h], p, 2 * ring(step) + core,
                        )
                    if step:
                        send()
                    else:
                        pl.when(core != k)(send)
    def spread_factor(which, n=0, of=1):
        size = coupling.shape[4] // of
        at = pl.ds(pl.multiple_of(n * size, size), size)
        for core in range(2):
            remote(
                factor(which, 0, 2 * core + 1).at[:, at], upp.at[which, k, :, at], upp_sent, upp_sem.at[which],
                4 * x + lax.rem(y + 1 + 2 * core, 4), 2 * z + core,
            )

    pl.when(p == 0)(lambda: spread_factor(INV))
    pl.when(both(even, p > 0))(lambda: spread_factor(C0))

    for which in (C0, INV, C1):
        @pl.when(odd)
        def _():
            lend(which, 0, mid, mid_sem, mid_sent)

        @pl.when(even if which == INV else both(even, p > 0))
        def _():
            remote(
                factor(which, 0, 2 * other), upp.at[which, k], upp_lent, upp_sem.at[which],
                p, 2 * z + other,
            )

        if which != C0:
            lend(which, 1, fac, fac_sem, fac_sent)

    def times(panel, ref):
        wide = jnp.concatenate([ref[0, 0], ref[1, 0], ref[0, 1], ref[1, 1]], axis=1)
        product = jnp.dot(panel, wide, preferred_element_type=F32)
        n = wide.shape[1] // 2
        real = product[:cut, :n] + product[cut:, n:]
        imag = product[cut:, :n] - product[:cut, n:]
        return jnp.concatenate([real, imag], axis=0)

    def across(ref, i):
        return jnp.concatenate([ref[i, chip] for chip in range(CHIPS)], axis=1)

    def place(i):
        g = lax.div(i, CUTS)
        q = lax.rem(i, CUTS)
        h = lax.div(q, CUTS // 2)
        r = lax.rem(q, CUTS // 2)
        return g, q, h, pl.multiple_of(r * cut, cut)

    def rows_of(q):
        return pl.ds(pl.multiple_of(q * cut, cut), cut)

    def odd_panel(i):
        g, _, h, r = place(i)
        parts = [
            jnp.concatenate([odd_v[g, h, col, part, pl.ds(r, cut)] for col in range(2 * CHIPS)], axis=1)
            for part in range(2)
        ]
        return jnp.concatenate(parts, axis=0)

    def along(ref, i, sent, sem):
        for step in (1, 3, 2):
            remote(ref.at[i, z], ref.at[i, z], sent, sem.at[i], p, 2 * ring(step) + k)

    def straight(src, dst, sent, got, column):
        for chip in range(CHIPS):
            remote(src, dst, sent, got, column, 2 * chip + k)

    def write_out(i, row, value):
        g, q, _, _ = place(i)
        at = rows_of(q)
        for side in range(2):
            for part in range(2):
                stage[side, g, row, part, at] = value[part * cut:(part + 1) * cut, side * 128:(side + 1) * 128]
        local(stage.at[k, g, row, :, at], out.at[2 * k + g, row, :, at], out_kept)
        remote(
            stage.at[other, g, row, :, at], out.at[2 * k + g, row, :, at], out_sent, out_sem,
            p, 2 * z + other,
        )

    def write_upper(j, value):
        at = rows_of(j)
        freq = 2 * k + up_g
        for side in range(2):
            for part in range(2):
                up_stage[side, part, at] = value[part * cut:(part + 1) * cut, side * 128:(side + 1) * 128]

        @pl.when(even)
        def _():
            local(up_stage.at[k, :, at], out.at[freq, 0, :, at], up_stage_kept)
            remote(
                up_stage.at[other, :, at], out.at[freq, 0, :, at], up_stage_sent, out_core_sem,
                p, 2 * z + other,
            )

        @pl.when(odd)
        def _():
            for side in range(2):
                remote(
                    up_stage.at[side, :, at], out.at[freq, 0, :, at], up_stage_sent, out_far_sem,
                    home, 2 * z + side,
                )

    def await_factor(ref, which, sem):
        for g in range(2):
            await_bytes(ref.at[which, g], sem.at[which, g])

    def await_upper(which):
        await_bytes(upp.at[which], upp_sem.at[which])

    def once(i, work):
        pl.when(i == 0)(work)

    def reduce_odd(i):
        g, q, h, _ = place(i)

        @pl.when(lax.rem(q, CUTS // 2) == 0)
        def _():
            await_bytes(odd_v.at[g, h], odd_sem.at[g, h])

        at = rows_of(q)
        mine = jnp.concatenate(
            [
                jnp.concatenate([even_f[side, g, part, at] for side in range(2)], axis=1)
                for part in range(2)
            ],
            axis=0,
        )
        left = (mine.astype(F32) - times(odd_panel(i), fac.at[C0, g])).astype(BF16)

        @pl.when(odd)
        def _():
            base[i, z] = left
            along(base, i, base_sent, base_sem)

        @pl.when(both(even, g == 0))
        def _():
            up_base[q] = left

        @pl.when(both(even, g == 1))
        def _():
            shard[q] = left
            remote(shard.at[q], up_base.at[q], shard_sent, up_base_sem.at[q], beside, c)

    def reduce_middle(i):
        g, q, _, _ = place(i)
        once(i, lambda: await_factor(mid, C0, mid_sem))
        await_bytes(base.at[i, pl.ds(0, 3)], base_sem.at[i])
        mid_out[i] = times(across(base, i), mid.at[C0, g]).astype(BF16)

        @pl.when(g == 0)
        def _():
            remote(mid_out.at[i], up_mid.at[q], mid_out_sent, up_mid_sem.at[q], p - 1, c)

        @pl.when(both(g == 1, k == 0))
        def _():
            local(mid_out.at[i], up_mid.at[q], up_mid_sem.at[q])

        @pl.when(both(g == 1, k == 1))
        def _():
            remote(mid_out.at[i], up_mid.at[q], mid_out_sent, up_mid_sem.at[q], twin, c)

    def inverse_odd(i):
        g, _, _, _ = place(i)
        once(i, lambda: await_factor(fac, INV, fac_sem))
        inv_odd[i] = times(odd_panel(i), fac.at[INV, g])

    def inverse_middle(i):
        g, _, _, _ = place(i)
        once(i, lambda: await_factor(mid, INV, mid_sem))
        inv_even[i] = times(across(base, i), mid.at[INV, g])

    def settle_upper(j):
        @pl.when(odd)
        def _():
            await_bytes(up_base.at[j], up_base_sem.at[j])

        await_bytes(up_mid.at[j], up_mid_sem.at[j])
        up_all[j, z] = (up_base[j].astype(F32) - up_mid[j].astype(F32)).astype(BF16)
        along(up_all, j, up_all_sent, up_all_sem)

    def reduce_upper(j):
        once(j, lambda: pl.when(inner)(lambda: await_upper(C0)))
        once(j, lambda: pl.when(top)(lambda: await_upper(INV)))
        await_bytes(up_all.at[j, pl.ds(0, 3)], up_all_sem.at[j])

        @pl.when(height == 0)
        def _():
            up_red[j] = up_all[j]

        for level in range(3):
            @pl.when(level < height)
            def _():
                await_bytes(up_upd.at[level, j], up_upd_sem.at[level, j])
                before = up_all[j].astype(F32) if level == 0 else acc[...]
                acc[...] = before - up_upd[level, j].astype(F32)

        @pl.when(height > 0)
        def _():
            up_red[j] = acc[...].astype(BF16)

        product = times(across(up_red, j), upp.at[jnp.where(top, INV, C0)])

        @pl.when(inner)
        def _():
            up_out[j] = product.astype(BF16)
            straight(up_out.at[j], up_upd.at[height, j, z], up_out_sent, up_upd_sem.at[height, j], parent)

        @pl.when(top)
        def _():
            solved_upper(j, product)

    def inverse_upper(j):
        once(j, lambda: await_upper(INV))
        up_inv[j] = times(across(up_red, j), upp.at[INV])

    def solved_upper(j, value):
        i = up_g * CUTS + j
        panel = value.astype(BF16)
        up_own[j] = panel

        @pl.when(height > 0)
        def _():
            straight(up_own.at[j], up_low.at[j, z], up_first_sent, up_low_sem.at[j], first)

        @pl.when(both(kind_b, jnp.logical_not(child_here)))
        def _():
            straight(up_own.at[j], low.at[i, z], up_first_sent, low_sem.at[i], child)

        @pl.when(child_here)
        def _():
            low[i, z] = panel
            along(low, i, low_sent, low_sem)

        @pl.when(top)
        def _():
            remote(up_own.at[j], up_low.at[j, z], shard_out_sent.at[0], up_shard_sem.at[j], p + 4, c)

        @pl.when(a_even)
        def _():
            remote(up_own.at[j], up_low.at[j, z], shard_out_sent.at[1], up_shard_sem.at[j], twin, c)

        @pl.when(both(kind_a, jnp.logical_not(child_here)))
        def _():
            remote(up_own.at[j], low.at[i, z], shard_out_sent.at[2], low_shard_sem.at[i], child, c)

        @pl.when(odd)
        def _():
            remote(up_own.at[j], own.at[i, z], shard_out_sent.at[3], own_shard_sem.at[j], home, c)

        @pl.when(even)
        def _():
            own[i, z] = panel
            along(own, i, own_sent, own_sem)

        write_upper(j, value)

    def spread_upper(j):
        await_bytes(up_low.at[j, 0], up_shard_sem.at[j])
        along(up_low, j, up_low_sent, up_low_sem)

    def spread_low(i):
        @pl.when(jnp.logical_not(both(child_here, i >= CUTS)))
        def _():
            await_bytes(low.at[i, 0], low_shard_sem.at[i])
            along(low, i, low_sent, low_sem)

    def spread_own(j):
        await_bytes(own.at[CUTS + j, 0], own_shard_sem.at[j])
        along(own, CUTS + j, own_sent, own_sem)

    def back_upper(j):
        once(j, lambda: await_upper(C1))

        @pl.when(by_shard)
        def _():
            await_bytes(up_low.at[j, pl.ds(0, 3)], up_low_sem.at[j])

        @pl.when(jnp.logical_not(by_shard))
        def _():
            await_bytes(up_low.at[j], up_low_sem.at[j])

        solved_upper(j, up_inv[j] - times(across(up_low, j), upp.at[C1]))

    def back_middle(i):
        g, _, _, _ = place(i)
        once(i, lambda: await_factor(mid, C1, mid_sem))
        whole = both(y == 3, jnp.logical_not(both(child_here, g == 1)))

        @pl.when(whole)
        def _():
            await_bytes(low.at[i], low_sem.at[i])

        @pl.when(jnp.logical_not(whole))
        def _():
            await_bytes(low.at[i, pl.ds(0, 3)], low_sem.at[i])

        value = inv_even[i] - times(across(low, i), mid.at[C1, g])
        own[i, z] = value.astype(BF16)
        along(own, i, own_sent, own_sem)
        write_out(i, 0, value)

    def back_odd(i):
        g, _, _, _ = place(i)
        once(i, lambda: await_factor(fac, C1, fac_sem))

        await_bytes(own.at[i, pl.ds(0, 3)], own_sem.at[i])
        write_out(i, 1, inv_odd[i] - times(across(own, i), fac.at[C1, g]))

    at_settle = jnp.where(even, MIDDLE + 3, MIDDLE + 7)
    at_upper = at_settle + jnp.where(kind_b, SETTLE, CUTS)
    at_middle_inverse = MIDDLE + 7 + 2 * CUTS
    at_back = at_middle_inverse + chunks + CUTS
    at_end = at_back + SETTLE + 3

    for g in range(2):
        await_bytes(fac.at[C0, g], fac_sem.at[C0, g])
    await_bytes(even_f, even_sem)

    def step(s, _):
        def during(start, count, work, who=None):
            i = s - start
            now = both(i >= 0, i < count)

            @pl.when(now if who is None else both(now, who))
            def _():
                work(i)

        during(0, chunks, reduce_odd)
        during(CUTS, PIECES, lambda n: spread_factor(INV, n, PIECES), both(even, p > 0))
        during(CUTS + PIECES, PIECES, lambda n: spread_factor(C1, n, PIECES), both(even, p > 0))
        during(MIDDLE, chunks, reduce_middle, odd)
        during(MIDDLE + 1, chunks, inverse_odd)
        during(at_settle, CUTS, settle_upper)
        during(at_upper, CUTS, reduce_upper)
        during(jnp.where(even, at_upper, at_back - CUTS), CUTS, inverse_upper, inner)
        during(at_middle_inverse, chunks, inverse_middle, odd)
        during(at_back, CUTS, spread_upper, by_shard)
        during(at_back + SETTLE, CUTS, back_upper, inner)
        during(at_back, chunks, spread_low, y == 1)
        during(at_back + SETTLE, chunks, back_middle, odd)
        during(at_back + SETTLE + CUTS, CUTS, spread_own, even)
        during(at_end, chunks, back_odd)
        return 0

    lax.fori_loop(0, at_end + chunks, step, 0)

    await_bytes(fac.at[:, 0], fac_sent)
    await_bytes(odd_v.at[:, :, pl.ds(0, 7)], odd_sent)
    await_bytes(even_f.at[0], even_sent)
    await_bytes(up_all.at[:, pl.ds(0, 3)], up_all_sent)
    await_bytes(own.at[:, pl.ds(0, 3)], own_sent)

    @pl.when(inner)
    def _():
        await_bytes(up_all, up_out_sent)

    @pl.when(jnp.logical_not(both(kind_b, child_here)))
    def _():
        await_bytes(up_all, up_first_sent)

    @pl.when(top)
    def _():
        await_bytes(up_own, shard_out_sent.at[0])

    @pl.when(a_even)
    def _():
        await_bytes(up_own, shard_out_sent.at[1])

    @pl.when(both(kind_a, jnp.logical_not(child_here)))
    def _():
        await_bytes(up_own, shard_out_sent.at[2])

    @pl.when(odd)
    def _():
        await_bytes(mid.at[:, 0], mid_sent)
        await_bytes(base.at[:, pl.ds(0, 3)], base_sent)
        await_bytes(up_own, shard_out_sent.at[3])
        await_bytes(stage.at[0], out_kept)
        await_bytes(stage.at[0], out_sent)
        await_bytes(stage.at[0], out_sem)
        await_bytes(up_stage, up_stage_sent)

    @pl.when(by_shard)
    def _():
        await_bytes(up_low.at[:, pl.ds(0, 3)], up_low_sent)

    @pl.when(y == 1)
    def _():
        await_bytes(low.at[:, pl.ds(0, 3)], low_sent)

    @pl.when(both(y == 3, k == 0))
    def _():
        await_bytes(low.at[pl.ds(0, CUTS), pl.ds(0, 3)], low_sent)

    @pl.when(both(odd, k == 0))
    def _():
        await_bytes(mid_out.at[pl.ds(0, CUTS)], mid_out_sent)

    @pl.when(both(odd, k == 1))
    def _():
        await_bytes(mid_out, mid_out_sent)

    @pl.when(p == 0)
    def _():
        await_bytes(upp.at[INV], upp_sent)
        await_bytes(upp.at[INV, 0], upp_lent)

    @pl.when(both(even, p > 0))
    def _():
        await_bytes(upp, upp_sent)
        await_bytes(upp.at[:, 0], upp_lent)

    @pl.when(even)
    def _():
        await_bytes(shard, shard_sent)
        await_bytes(stage.at[0, 0], out_kept)
        await_bytes(stage.at[0, 0], out_sent)
        await_bytes(stage.at[0, 0], out_sem)
        await_bytes(up_stage.at[0], up_stage_kept)
        await_bytes(up_stage.at[0], up_stage_sent)
        await_bytes(up_stage.at[0], out_core_sem)
        await_bytes(up_stage, out_far_sem)


def local_solve(force, inverse, coupling):
    rhs, cols = force.shape[3:]
    block = inverse.shape[3]
    chunks = 2 * CUTS
    rows = 2 * rhs // CUTS
    wide = 2 * cols
    dma = pltpu.SemaphoreType.DMA
    piece = (rows, wide)
    panel = (chunks, CHIPS) + piece
    upper = (CUTS, CHIPS) + piece
    weight = (2, 2, block, cols)
    hbm = pl.BlockSpec(memory_space=pl.ANY)
    return pl.pallas_call(
        kernel,
        out_shape=jax.ShapeDtypeStruct(force.shape, F32),
        in_specs=[hbm] * 3,
        out_specs=hbm,
        scratch_shapes=[
            pltpu.VMEM((3, 2) + weight, BF16),
            pltpu.VMEM((3, 2) + weight, BF16),
            pltpu.VMEM((3,) + weight, BF16),
            pltpu.VMEM((2, 2, 2 * CHIPS, 2, rhs // 2, cols), BF16),
            pltpu.VMEM((2, 2, 2, rhs, cols), BF16),
            pltpu.VMEM(panel, BF16),
            pltpu.VMEM((CUTS,) + piece, BF16),
            pltpu.VMEM((chunks,) + piece, BF16),
            pltpu.VMEM((CUTS,) + piece, BF16),
            pltpu.VMEM((CUTS,) + piece, BF16),
            pltpu.VMEM(upper, BF16),
            pltpu.VMEM((3,) + upper, BF16),
            pltpu.VMEM((CUTS,) + piece, BF16),
            pltpu.VMEM(upper, BF16),
            pltpu.VMEM((CUTS,) + piece, F32),
            pltpu.VMEM(upper, BF16),
            pltpu.VMEM((CUTS,) + piece, BF16),
            pltpu.VMEM((chunks,) + piece, F32),
            pltpu.VMEM((chunks,) + piece, F32),
            pltpu.VMEM(panel, BF16),
            pltpu.VMEM(panel, BF16),
            pltpu.VMEM((2, 2, 2, 2, rhs, cols), F32),
            pltpu.VMEM((2, 2, rhs, cols), F32),
            pltpu.VMEM((CHIPS,) + piece, F32),
            dma((3, 2)), dma((3, 2)), dma((3,)), dma((2, 2)), dma, dma((chunks,)), dma((CUTS,)), dma((CUTS,)),
            dma((CUTS,)), dma((3, CUTS)), dma((CUTS,)), dma((chunks,)), dma((chunks,)), dma((CUTS,)),
            dma((chunks,)), dma((CUTS,)), dma, dma, dma,
            dma, dma, dma, dma, dma, dma, dma, dma, dma, dma, dma, dma, dma((4,)), dma, dma, dma, dma, dma, dma, dma,
        ],
        compiler_params=pltpu.CompilerParams(
            collective_id=0, has_side_effects=True, vmem_limit_bytes=60 * 2**20
        ),
        name="resolvent",
    )(force, inverse, coupling)


def solution(mesh):
    return jax.shard_map(
        local_solve,
        mesh=mesh,
        in_specs=(
            P(None, "radial", None, None, "col"),
            P(None, "radial", None, None, "col"),
            P(None, "radial", None, None, None, "col"),
        ),
        out_specs=P(None, "radial", None, None, "col"),
        check_vma=False,
    )
```

```python
import jax
import jax.numpy as jnp
from jax import lax
from jax.experimental import pallas as pl
from jax.experimental.pallas import tpu as pltpu
from jax.sharding import PartitionSpec as P

MESH = pl.DeviceIdType.MESH
BF16 = jnp.bfloat16
F32 = jnp.float32
CHIPS = 4
CUTS = 4
C0, INV, C1 = range(3)
MIDDLE = 3
SETTLE = 2
AHEAD = 4
PIECE_CORE = [0, 0, 1, 0, 1, 0, 1, 1]
PIECE_OF_CORE = [0, 1, 0, 2, 1, 3, 2, 3]
PIECES = 8


def kernel(
    force, inverse, coupling, out,
    fac, mid, upp, odd_v, even_f, base, shard, mid_out, up_base, up_mid, up_all, up_upd, up_out, up_red,
    up_inv, up_low, up_own, inv_even, inv_odd, low, own, stage, up_stage, acc,
    fac_sem, mid_sem, upp_sem, odd_sem, even_sem, base_sem, up_base_sem, up_mid_sem, up_all_sem, up_upd_sem,
    up_low_sem, low_sem, own_sem, up_shard_sem, low_shard_sem, own_shard_sem, out_sem, out_core_sem, out_far_sem,
    fac_sent, mid_sent, upp_lent, upp_sent, odd_sent, even_sent, base_sent, shard_sent, mid_out_sent,
    up_all_sent, up_out_sent, up_first_sent, shard_out_sent, up_low_sent, low_sent, own_sent, out_sent, out_kept,
    up_stage_sent, up_stage_kept,
):
    chunks = base.shape[0]
    rhs = force.shape[3]
    cut = rhs // CUTS
    half = rhs // 2
    p = lax.axis_index("radial")
    c = lax.axis_index("col")
    x, y = lax.div(p, 4), lax.rem(p, 4)
    z, k = lax.div(c, 2), lax.rem(c, 2)
    other = 1 - k
    odd = lax.rem(y, 2) == 1
    even = lax.rem(y, 2) == 0
    kind_a = jnp.logical_or(y == 0, jnp.logical_and(odd, y == 1 + 2 * k))
    kind_b = jnp.logical_not(kind_a)
    up_g = lax.rem(y, 2)
    home = 4 * x + jnp.where(kind_a, 0, 2)
    height = jnp.where(kind_b, 0, jnp.where(lax.rem(x, 2) == 1, 1, jnp.where(x == 2, 2, 3)))
    top = height == 3
    inner = height < 3
    twin = 4 * x + lax.rem(y + 2, 4)
    parent = jnp.where(kind_b, twin, jnp.where(height == 1, p - 4, jnp.where(height == 2, p - 8, p)))
    first = jnp.where(height == 3, p + 8, jnp.where(height == 2, p + 4, twin))
    beside = 4 * x + lax.rem(y + 1 + 2 * k, 4)
    child = 4 * x + jnp.where(kind_a, 1, 3)
    child_here = child == p
    by_shard = jnp.logical_or(jnp.logical_and(height == 1, x == 1), jnp.logical_and(kind_b, lax.rem(x, 2) == 0))

    def both(one, two):
        return jnp.logical_and(one, two)

    def ring(step):
        return lax.rem(z + step, CHIPS)

    def remote(src, dst, sent, got, column, target):
        pltpu.make_async_remote_copy(
            src_ref=src, dst_ref=dst, send_sem=sent, recv_sem=got,
            device_id=(column, target), device_id_type=MESH,
        ).start()

    def local(src, dst, sem):
        pltpu.make_async_copy(src, dst, sem).start()

    def await_bytes(ref, sem):
        pltpu.make_async_copy(ref, ref, sem).wait()

    def factor(which, row, freq):
        if which == INV:
            return inverse.at[freq, row]
        return coupling.at[freq, row, 0 if which == C0 else 1]

    def keep(which, row, ref, sem):
        for g in range(2):
            local(factor(which, row, 2 * k + g), ref.at[which, g, k], sem.at[which, g])

    def lend(which, row, ref, sem, sent):
        for g in range(2):
            remote(
                factor(which, row, 2 * other + g), ref.at[which, g, k], sent, sem.at[which, g],
                p, 2 * z + other,
            )

    keep(C0, 1, fac, fac_sem)
    local(force.at[pl.ds(2 * k, 2), 0], even_f.at[k], even_sem)
    for g in range(2):
        for h in range(2):
            local(
                force.at[2 * k + g, 1, :, pl.ds(h * half, half)], odd_v.at[g, h, c], odd_sem.at[g, h]
            )
    for which in (C0, INV, C1):
        @pl.when(odd)
        def _():
            keep(which, 0, mid, mid_sem)

        @pl.when(even if which == INV else both(even, p > 0))
        def _():
            local(factor(which, 0, 2 * k), upp.at[which, k], upp_sem.at[which])

        if which != C0:
            keep(which, 1, fac, fac_sem)

    barrier = pltpu.get_barrier_semaphore()

    def greet(column, target):
        pl.semaphore_signal(barrier, inc=1, device_id=(column, target), device_id_type=MESH)

    for step in range(1, CHIPS):
        for core in range(2):
            greet(p, 2 * ring(step) + core)
    greet(p, 2 * z + other)
    for core in range(2):
        greet(4 * x + lax.rem(y + 1, 4), 2 * z + core)
        greet(4 * x + lax.rem(y + 3, 4), 2 * z + core)
    for chip in range(CHIPS):
        greet(twin, 2 * chip + k)

    @pl.when(y >= 2)
    def _():
        for step in range(1, CHIPS):
            greet(4 * x + 5 - y, 2 * ring(step) + k)

    def greet_chips(column):
        for chip in range(CHIPS):
            greet(column, 2 * chip + k)

    a_even = both(kind_a, lax.rem(x, 2) == 0)

    @pl.when(both(kind_a, height < 3))
    def _():
        greet_chips(parent)

    @pl.when(a_even)
    def _():
        greet_chips(p + 4)

    @pl.when(top)
    def _():
        greet_chips(p + 8)

    pl.semaphore_wait(
        barrier,
        15 + jnp.where(y >= 2, 3, 0) + jnp.where(kind_a, jnp.where(lax.rem(x, 2) == 0, 8, 4), 0),
    )

    lend(C0, 1, fac, fac_sem, fac_sent)
    remote(force.at[pl.ds(2 * other, 2), 0], even_f.at[k], even_sent, even_sem, p, 2 * z + other)
    def pick(n, values):
        found = values[-1]
        for at in range(len(values) - 1):
            found = jnp.where(n == at, values[at], found)
        return found

    def send_odd(n, _):
        core, piece = pick(n, PIECE_CORE), pick(n, PIECE_OF_CORE)
        g, h = lax.div(piece, 2), lax.rem(piece, 2)
        src = force.at[2 * core + g, 1, :, pl.ds(pl.multiple_of(h * half, half), half)]
        for step in (2, 1, 3):
            remote(src, odd_v.at[g, h, c], odd_sent, odd_sem.at[g, h], p, 2 * ring(step) + core)

        @pl.when(core != k)
        def _():
            remote(src, odd_v.at[g, h, c], odd_sent, odd_sem.at[g, h], p, 2 * z + core)

        return 0

    def allowed(piece):
        come = jnp.where(
            k == 0, pick(piece, [n for n in range(8) if PIECE_CORE[n] == 0]),
            pick(piece, [n for n in range(8) if PIECE_CORE[n] == 1]),
        )
        return jnp.minimum(come + 1 + AHEAD, 8)

    lax.fori_loop(0, AHEAD, send_odd, 0)

    def spread_factor(which, n=0, of=1):
        size = coupling.shape[4] // of
        at = pl.ds(pl.multiple_of(n * size, size), size)
        for core in range(2):
            remote(
                factor(which, 0, 2 * core + 1).at[:, at], upp.at[which, k, :, at], upp_sent, upp_sem.at[which],
                4 * x + lax.rem(y + 1 + 2 * core, 4), 2 * z + core,
            )

    pl.when(p == 0)(lambda: spread_factor(INV))
    pl.when(both(even, p > 0))(lambda: spread_factor(C0))

    for which in (C0, INV, C1):
        @pl.when(odd)
        def _():
            lend(which, 0, mid, mid_sem, mid_sent)

        @pl.when(even if which == INV else both(even, p > 0))
        def _():
            remote(
                factor(which, 0, 2 * other), upp.at[which, k], upp_lent, upp_sem.at[which],
                p, 2 * z + other,
            )

        if which != C0:
            lend(which, 1, fac, fac_sem, fac_sent)

    def times(panel, ref):
        wide = jnp.concatenate([ref[0, 0], ref[1, 0], ref[0, 1], ref[1, 1]], axis=1)
        product = jnp.dot(panel, wide, preferred_element_type=F32)
        n = wide.shape[1] // 2
        real = product[:cut, :n] + product[cut:, n:]
        imag = product[cut:, :n] - product[:cut, n:]
        return jnp.concatenate([real, imag], axis=0)

    def across(ref, i):
        return jnp.concatenate([ref[i, chip] for chip in range(CHIPS)], axis=1)

    def place(i):
        g = lax.div(i, CUTS)
        q = lax.rem(i, CUTS)
        h = lax.div(q, CUTS // 2)
        r = lax.rem(q, CUTS // 2)
        return g, q, h, pl.multiple_of(r * cut, cut)

    def rows_of(q):
        return pl.ds(pl.multiple_of(q * cut, cut), cut)

    def odd_panel(i):
        g, _, h, r = place(i)
        parts = [
            jnp.concatenate([odd_v[g, h, col, part, pl.ds(r, cut)] for col in range(2 * CHIPS)], axis=1)
            for part in range(2)
        ]
        return jnp.concatenate(parts, axis=0)

    def along(ref, i, sent, sem):
        for step in (1, 3, 2):
            remote(ref.at[i, z], ref.at[i, z], sent, sem.at[i], p, 2 * ring(step) + k)

    def straight(src, dst, sent, got, column):
        for step in (2, 1, 3, 0):
            remote(src, dst, sent, got, column, 2 * ring(step) + k)

    def write_out(i, row, value):
        g, q, _, _ = place(i)
        at = rows_of(q)
        for side in range(2):
            for part in range(2):
                stage[side, g, row, part, at] = value[part * cut:(part + 1) * cut, side * 128:(side + 1) * 128]
        local(stage.at[k, g, row, :, at], out.at[2 * k + g, row, :, at], out_kept)
        remote(
            stage.at[other, g, row, :, at], out.at[2 * k + g, row, :, at], out_sent, out_sem,
            p, 2 * z + other,
        )

    def write_upper(j, value):
        at = rows_of(j)
        freq = 2 * k + up_g
        for side in range(2):
            for part in range(2):
                up_stage[side, part, at] = value[part * cut:(part + 1) * cut, side * 128:(side + 1) * 128]

        @pl.when(even)
        def _():
            local(up_stage.at[k, :, at], out.at[freq, 0, :, at], up_stage_kept)
            remote(
                up_stage.at[other, :, at], out.at[freq, 0, :, at], up_stage_sent, out_core_sem,
                p, 2 * z + other,
            )

        @pl.when(odd)
        def _():
            for side in range(2):
                remote(
                    up_stage.at[side, :, at], out.at[freq, 0, :, at], up_stage_sent, out_far_sem,
                    home, 2 * z + side,
                )

    def await_factor(ref, which, sem):
        for g in range(2):
            await_bytes(ref.at[which, g], sem.at[which, g])

    def await_upper(which):
        await_bytes(upp.at[which], upp_sem.at[which])

    def once(i, work):
        pl.when(i == 0)(work)

    def reduce_odd(i):
        g, q, h, _ = place(i)

        @pl.when(lax.rem(q, CUTS // 2) == 0)
        def _():
            await_bytes(odd_v.at[g, h], odd_sem.at[g, h])
            piece = 2 * g + h
            sent = jnp.where(piece == 0, AHEAD, allowed(piece - 1))
            lax.fori_loop(sent, jnp.where(piece == 3, 8, allowed(piece)), send_odd, 0)

        at = rows_of(q)
        mine = jnp.concatenate(
            [
                jnp.concatenate([even_f[side, g, part, at] for side in range(2)], axis=1)
                for part in range(2)
            ],
            axis=0,
        )
        left = (mine.astype(F32) - times(odd_panel(i), fac.at[C0, g])).astype(BF16)

        @pl.when(odd)
        def _():
            base[i, z] = left
            along(base, i, base_sent, base_sem)

        @pl.when(both(even, g == 0))
        def _():
            up_base[q] = left

        @pl.when(both(even, g == 1))
        def _():
            shard[q] = left
            remote(shard.at[q], up_base.at[q], shard_sent, up_base_sem.at[q], beside, c)

    def reduce_middle(i):
        g, q, _, _ = place(i)
        once(i, lambda: await_factor(mid, C0, mid_sem))
        await_bytes(base.at[i, pl.ds(0, 3)], base_sem.at[i])
        mid_out[i] = times(across(base, i), mid.at[C0, g]).astype(BF16)

        @pl.when(g == 0)
        def _():
            remote(mid_out.at[i], up_mid.at[q], mid_out_sent, up_mid_sem.at[q], p - 1, c)

        @pl.when(both(g == 1, k == 0))
        def _():
            local(mid_out.at[i], up_mid.at[q], up_mid_sem.at[q])

        @pl.when(both(g == 1, k == 1))
        def _():
            remote(mid_out.at[i], up_mid.at[q], mid_out_sent, up_mid_sem.at[q], twin, c)

    def inverse_odd(i):
        g, _, _, _ = place(i)
        once(i, lambda: await_factor(fac, INV, fac_sem))
        inv_odd[i] = times(odd_panel(i), fac.at[INV, g])

    def inverse_middle(i):
        g, _, _, _ = place(i)
        once(i, lambda: await_factor(mid, INV, mid_sem))
        inv_even[i] = times(across(base, i), mid.at[INV, g])

    def settle_upper(j):
        @pl.when(odd)
        def _():
            await_bytes(up_base.at[j], up_base_sem.at[j])

        await_bytes(up_mid.at[j], up_mid_sem.at[j])
        up_all[j, z] = (up_base[j].astype(F32) - up_mid[j].astype(F32)).astype(BF16)
        along(up_all, j, up_all_sent, up_all_sem)

    def reduce_upper(j):
        once(j, lambda: pl.when(inner)(lambda: await_upper(C0)))
        once(j, lambda: pl.when(top)(lambda: await_upper(INV)))
        await_bytes(up_all.at[j, pl.ds(0, 3)], up_all_sem.at[j])

        @pl.when(height == 0)
        def _():
            up_red[j] = up_all[j]

        for level in range(3):
            @pl.when(level < height)
            def _():
                await_bytes(up_upd.at[level, j], up_upd_sem.at[level, j])
                before = up_all[j].astype(F32) if level == 0 else acc[...]
                acc[...] = before - up_upd[level, j].astype(F32)

        @pl.when(height > 0)
        def _():
            up_red[j] = acc[...].astype(BF16)

        product = times(across(up_red, j), upp.at[jnp.where(top, INV, C0)])

        @pl.when(inner)
        def _():
            up_out[j] = product.astype(BF16)
            straight(up_out.at[j], up_upd.at[height, j, z], up_out_sent, up_upd_sem.at[height, j], parent)

        @pl.when(top)
        def _():
            solved_upper(j, product)

    def inverse_upper(j):
        once(j, lambda: await_upper(INV))
        up_inv[j] = times(across(up_red, j), upp.at[INV])

    def solved_upper(j, value):
        i = up_g * CUTS + j
        panel = value.astype(BF16)
        up_own[j] = panel

        @pl.when(height > 0)
        def _():
            straight(up_own.at[j], up_low.at[j, z], up_first_sent, up_low_sem.at[j], first)

        @pl.when(both(kind_b, jnp.logical_not(child_here)))
        def _():
            straight(up_own.at[j], low.at[i, z], up_first_sent, low_sem.at[i], child)

        @pl.when(child_here)
        def _():
            low[i, z] = panel
            along(low, i, low_sent, low_sem)

        @pl.when(top)
        def _():
            remote(up_own.at[j], up_low.at[j, z], shard_out_sent.at[0], up_shard_sem.at[j], p + 4, c)

        @pl.when(a_even)
        def _():
            remote(up_own.at[j], up_low.at[j, z], shard_out_sent.at[1], up_shard_sem.at[j], twin, c)

        @pl.when(both(kind_a, jnp.logical_not(child_here)))
        def _():
            remote(up_own.at[j], low.at[i, z], shard_out_sent.at[2], low_shard_sem.at[i], child, c)

        @pl.when(odd)
        def _():
            remote(up_own.at[j], own.at[i, z], shard_out_sent.at[3], own_shard_sem.at[j], home, c)

        @pl.when(even)
        def _():
            own[i, z] = panel
            along(own, i, own_sent, own_sem)

        write_upper(j, value)

    def spread_upper(j):
        await_bytes(up_low.at[j, 0], up_shard_sem.at[j])
        along(up_low, j, up_low_sent, up_low_sem)

    def spread_low(i):
        @pl.when(jnp.logical_not(both(child_here, i >= CUTS)))
        def _():
            await_bytes(low.at[i, 0], low_shard_sem.at[i])
            along(low, i, low_sent, low_sem)

    def spread_own(j):
        await_bytes(own.at[CUTS + j, 0], own_shard_sem.at[j])
        along(own, CUTS + j, own_sent, own_sem)

    def back_upper(j):
        once(j, lambda: await_upper(C1))

        @pl.when(by_shard)
        def _():
            await_bytes(up_low.at[j, pl.ds(0, 3)], up_low_sem.at[j])

        @pl.when(jnp.logical_not(by_shard))
        def _():
            await_bytes(up_low.at[j], up_low_sem.at[j])

        solved_upper(j, up_inv[j] - times(across(up_low, j), upp.at[C1]))

    def back_middle(i):
        g, _, _, _ = place(i)
        once(i, lambda: await_factor(mid, C1, mid_sem))
        whole = both(y == 3, jnp.logical_not(both(child_here, g == 1)))

        @pl.when(whole)
        def _():
            await_bytes(low.at[i], low_sem.at[i])

        @pl.when(jnp.logical_not(whole))
        def _():
            await_bytes(low.at[i, pl.ds(0, 3)], low_sem.at[i])

        value = inv_even[i] - times(across(low, i), mid.at[C1, g])
        own[i, z] = value.astype(BF16)
        along(own, i, own_sent, own_sem)
        write_out(i, 0, value)

    def back_odd(i):
        g, _, _, _ = place(i)
        once(i, lambda: await_factor(fac, C1, fac_sem))

        await_bytes(own.at[i, pl.ds(0, 3)], own_sem.at[i])
        write_out(i, 1, inv_odd[i] - times(across(own, i), fac.at[C1, g]))

    at_settle = jnp.where(even, MIDDLE + 3, MIDDLE + 7)
    at_upper = at_settle + jnp.where(kind_b, SETTLE, CUTS)
    at_middle_inverse = MIDDLE + 7 + 2 * CUTS
    at_back = at_middle_inverse + chunks + CUTS
    at_end = at_back + SETTLE + 3

    for g in range(2):
        await_bytes(fac.at[C0, g], fac_sem.at[C0, g])
    await_bytes(even_f, even_sem)

    def step(s, _):
        def during(start, count, work, who=None):
            i = s - start
            now = both(i >= 0, i < count)

            @pl.when(now if who is None else both(now, who))
            def _():
                work(i)

        during(0, chunks, reduce_odd)
        at_move = jnp.where(kind_a, CUTS, MIDDLE + 3 + SETTLE + CUTS)
        during(at_move, PIECES, lambda n: spread_factor(INV, n, PIECES), both(even, p > 0))
        during(at_move + PIECES, PIECES, lambda n: spread_factor(C1, n, PIECES), both(even, p > 0))
        during(MIDDLE, chunks, reduce_middle, odd)
        during(MIDDLE + 1, chunks, inverse_odd)
        during(at_settle, CUTS, settle_upper)
        during(at_upper, CUTS, reduce_upper)
        during(jnp.where(even, at_upper, at_back - CUTS), CUTS, inverse_upper, inner)
        during(at_middle_inverse, chunks, inverse_middle, odd)
        during(at_back, CUTS, spread_upper, by_shard)
        during(at_back + SETTLE, CUTS, back_upper, inner)
        during(at_back, chunks, spread_low, y == 1)
        during(at_back + SETTLE, chunks, back_middle, odd)
        during(at_back + SETTLE + CUTS, CUTS, spread_own, even)
        during(at_end, chunks, back_odd)
        return 0

    lax.fori_loop(0, at_end + chunks, step, 0)

    await_bytes(fac.at[:, 0], fac_sent)
    await_bytes(odd_v.at[:, :, pl.ds(0, 7)], odd_sent)
    await_bytes(even_f.at[0], even_sent)
    await_bytes(up_all.at[:, pl.ds(0, 3)], up_all_sent)
    await_bytes(own.at[:, pl.ds(0, 3)], own_sent)

    @pl.when(inner)
    def _():
        await_bytes(up_all, up_out_sent)

    @pl.when(jnp.logical_not(both(kind_b, child_here)))
    def _():
        await_bytes(up_all, up_first_sent)

    @pl.when(top)
    def _():
        await_bytes(up_own, shard_out_sent.at[0])

    @pl.when(a_even)
    def _():
        await_bytes(up_own, shard_out_sent.at[1])

    @pl.when(both(kind_a, jnp.logical_not(child_here)))
    def _():
        await_bytes(up_own, shard_out_sent.at[2])

    @pl.when(odd)
    def _():
        await_bytes(mid.at[:, 0], mid_sent)
        await_bytes(base.at[:, pl.ds(0, 3)], base_sent)
        await_bytes(up_own, shard_out_sent.at[3])
        await_bytes(stage.at[0], out_kept)
        await_bytes(stage.at[0], out_sent)
        await_bytes(stage.at[0], out_sem)
        await_bytes(up_stage, up_stage_sent)

    @pl.when(by_shard)
    def _():
        await_bytes(up_low.at[:, pl.ds(0, 3)], up_low_sent)

    @pl.when(y == 1)
    def _():
        await_bytes(low.at[:, pl.ds(0, 3)], low_sent)

    @pl.when(both(y == 3, k == 0))
    def _():
        await_bytes(low.at[pl.ds(0, CUTS), pl.ds(0, 3)], low_sent)

    @pl.when(both(odd, k == 0))
    def _():
        await_bytes(mid_out.at[pl.ds(0, CUTS)], mid_out_sent)

    @pl.when(both(odd, k == 1))
    def _():
        await_bytes(mid_out, mid_out_sent)

    @pl.when(p == 0)
    def _():
        await_bytes(upp.at[INV], upp_sent)
        await_bytes(upp.at[INV, 0], upp_lent)

    @pl.when(both(even, p > 0))
    def _():
        await_bytes(upp, upp_sent)
        await_bytes(upp.at[:, 0], upp_lent)

    @pl.when(even)
    def _():
        await_bytes(shard, shard_sent)
        await_bytes(stage.at[0, 0], out_kept)
        await_bytes(stage.at[0, 0], out_sent)
        await_bytes(stage.at[0, 0], out_sem)
        await_bytes(up_stage.at[0], up_stage_kept)
        await_bytes(up_stage.at[0], up_stage_sent)
        await_bytes(up_stage.at[0], out_core_sem)
        await_bytes(up_stage, out_far_sem)


def local_solve(force, inverse, coupling):
    rhs, cols = force.shape[3:]
    block = inverse.shape[3]
    chunks = 2 * CUTS
    rows = 2 * rhs // CUTS
    wide = 2 * cols
    dma = pltpu.SemaphoreType.DMA
    piece = (rows, wide)
    panel = (chunks, CHIPS) + piece
    upper = (CUTS, CHIPS) + piece
    weight = (2, 2, block, cols)
    hbm = pl.BlockSpec(memory_space=pl.ANY)
    return pl.pallas_call(
        kernel,
        out_shape=jax.ShapeDtypeStruct(force.shape, F32),
        in_specs=[hbm] * 3,
        out_specs=hbm,
        scratch_shapes=[
            pltpu.VMEM((3, 2) + weight, BF16),
            pltpu.VMEM((3, 2) + weight, BF16),
            pltpu.VMEM((3,) + weight, BF16),
            pltpu.VMEM((2, 2, 2 * CHIPS, 2, rhs // 2, cols), BF16),
            pltpu.VMEM((2, 2, 2, rhs, cols), BF16),
            pltpu.VMEM(panel, BF16),
            pltpu.VMEM((CUTS,) + piece, BF16),
            pltpu.VMEM((chunks,) + piece, BF16),
            pltpu.VMEM((CUTS,) + piece, BF16),
            pltpu.VMEM((CUTS,) + piece, BF16),
            pltpu.VMEM(upper, BF16),
            pltpu.VMEM((3,) + upper, BF16),
            pltpu.VMEM((CUTS,) + piece, BF16),
            pltpu.VMEM(upper, BF16),
            pltpu.VMEM((CUTS,) + piece, F32),
            pltpu.VMEM(upper, BF16),
            pltpu.VMEM((CUTS,) + piece, BF16),
            pltpu.VMEM((chunks,) + piece, F32),
            pltpu.VMEM((chunks,) + piece, F32),
            pltpu.VMEM(panel, BF16),
            pltpu.VMEM(panel, BF16),
            pltpu.VMEM((2, 2, 2, 2, rhs, cols), F32),
            pltpu.VMEM((2, 2, rhs, cols), F32),
            pltpu.VMEM((CHIPS,) + piece, F32),
            dma((3, 2)), dma((3, 2)), dma((3,)), dma((2, 2)), dma, dma((chunks,)), dma((CUTS,)), dma((CUTS,)),
            dma((CUTS,)), dma((3, CUTS)), dma((CUTS,)), dma((chunks,)), dma((chunks,)), dma((CUTS,)),
            dma((chunks,)), dma((CUTS,)), dma, dma, dma,
            dma, dma, dma, dma, dma, dma, dma, dma, dma, dma, dma, dma, dma((4,)), dma, dma, dma, dma, dma, dma, dma,
        ],
        compiler_params=pltpu.CompilerParams(
            collective_id=0, has_side_effects=True, vmem_limit_bytes=60 * 2**20
        ),
        name="resolvent",
    )(force, inverse, coupling)


def solution(mesh):
    return jax.shard_map(
        local_solve,
        mesh=mesh,
        in_specs=(
            P(None, "radial", None, None, "col"),
            P(None, "radial", None, None, "col"),
            P(None, "radial", None, None, None, "col"),
        ),
        out_specs=P(None, "radial", None, None, "col"),
        check_vma=False,
    )
```

```python
import jax
import jax.numpy as jnp
from jax import lax
from jax.experimental import pallas as pl
from jax.experimental.pallas import tpu as pltpu
from jax.sharding import PartitionSpec as P

MESH = pl.DeviceIdType.MESH
BF16 = jnp.bfloat16
F32 = jnp.float32
CHIPS = 4
CUTS = 4
C0, INV, C1 = range(3)
MIDDLE = 3
SETTLE = 2
AHEAD = 4
PIECE_CORE = [0, 0, 1, 0, 1, 0, 1, 1]
PIECE_OF_CORE = [0, 1, 0, 2, 1, 3, 2, 3]
PIECES = 8


def kernel(
    force, inverse, coupling, out,
    fac, mid, upp, odd_v, even_f, base, shard, mid_out, up_base, up_mid, up_all, up_upd, up_out, up_red,
    up_inv, up_low, up_own, inv_even, inv_odd, low, own, stage, up_stage, acc,
    fac_sem, mid_sem, upp_sem, odd_sem, even_sem, base_sem, up_base_sem, up_mid_sem, up_all_sem, up_upd_sem,
    up_low_sem, low_sem, own_sem, up_shard_sem, low_shard_sem, own_shard_sem, out_sem, out_core_sem, out_far_sem,
    fac_sent, mid_sent, upp_lent, upp_sent, odd_sent, even_sent, base_sent, shard_sent, mid_out_sent,
    up_all_sent, up_out_sent, up_first_sent, shard_out_sent, up_low_sent, low_sent, own_sent, out_sent, out_kept,
    up_stage_sent, up_stage_kept,
):
    chunks = base.shape[0]
    rhs = force.shape[3]
    cut = rhs // CUTS
    half = rhs // 2
    p = lax.axis_index("radial")
    c = lax.axis_index("col")
    x, y = lax.div(p, 4), lax.rem(p, 4)
    z, k = lax.div(c, 2), lax.rem(c, 2)
    other = 1 - k
    odd = lax.rem(y, 2) == 1
    even = lax.rem(y, 2) == 0
    kind_a = jnp.logical_or(y == 0, jnp.logical_and(odd, y == 1 + 2 * k))
    kind_b = jnp.logical_not(kind_a)
    up_g = lax.rem(y, 2)
    home = 4 * x + jnp.where(kind_a, 0, 2)
    height = jnp.where(kind_b, 0, jnp.where(lax.rem(x, 2) == 1, 1, jnp.where(x == 2, 2, 3)))
    top = height == 3
    inner = height < 3
    twin = 4 * x + lax.rem(y + 2, 4)
    parent = jnp.where(kind_b, twin, jnp.where(height == 1, p - 4, jnp.where(height == 2, p - 8, p)))
    first = jnp.where(height == 3, p + 8, jnp.where(height == 2, p + 4, twin))
    beside = 4 * x + lax.rem(y + 1 + 2 * k, 4)
    child = 4 * x + jnp.where(kind_a, 1, 3)
    child_here = child == p
    by_shard = jnp.logical_or(jnp.logical_and(height == 1, x == 1), jnp.logical_and(kind_b, lax.rem(x, 2) == 0))

    def both(one, two):
        return jnp.logical_and(one, two)

    def ring(step):
        return lax.rem(z + step, CHIPS)

    def remote(src, dst, sent, got, column, target):
        pltpu.make_async_remote_copy(
            src_ref=src, dst_ref=dst, send_sem=sent, recv_sem=got,
            device_id=(column, target), device_id_type=MESH,
        ).start()

    def local(src, dst, sem):
        pltpu.make_async_copy(src, dst, sem).start()

    def await_bytes(ref, sem):
        pltpu.make_async_copy(ref, ref, sem).wait()

    def factor(which, row, freq):
        if which == INV:
            return inverse.at[freq, row]
        return coupling.at[freq, row, 0 if which == C0 else 1]

    def keep(which, row, ref, sem):
        for g in range(2):
            local(factor(which, row, 2 * k + g), ref.at[which, g, k], sem.at[which, g])

    def lend(which, row, ref, sem, sent):
        for g in range(2):
            remote(
                factor(which, row, 2 * other + g), ref.at[which, g, k], sent, sem.at[which, g],
                p, 2 * z + other,
            )

    keep(C0, 1, fac, fac_sem)
    local(force.at[pl.ds(2 * k, 2), 0], even_f.at[k], even_sem)
    for g in range(2):
        for h in range(2):
            local(
                force.at[2 * k + g, 1, :, pl.ds(h * half, half)], odd_v.at[g, h, c], odd_sem.at[g, h]
            )
    for which in (C0, INV, C1):
        @pl.when(odd)
        def _():
            keep(which, 0, mid, mid_sem)

        @pl.when(even if which == INV else both(even, p > 0))
        def _():
            local(factor(which, 0, 2 * k), upp.at[which, k], upp_sem.at[which])

        if which != C0:
            keep(which, 1, fac, fac_sem)

    barrier = pltpu.get_barrier_semaphore()

    def greet(column, target):
        pl.semaphore_signal(barrier, inc=1, device_id=(column, target), device_id_type=MESH)

    for step in range(1, CHIPS):
        for core in range(2):
            greet(p, 2 * ring(step) + core)
    greet(p, 2 * z + other)
    for core in range(2):
        greet(4 * x + lax.rem(y + 1, 4), 2 * z + core)
        greet(4 * x + lax.rem(y + 3, 4), 2 * z + core)
    for chip in range(CHIPS):
        greet(twin, 2 * chip + k)

    @pl.when(y >= 2)
    def _():
        for step in range(1, CHIPS):
            greet(4 * x + 5 - y, 2 * ring(step) + k)

    def greet_chips(column):
        for chip in range(CHIPS):
            greet(column, 2 * chip + k)

    a_even = both(kind_a, lax.rem(x, 2) == 0)

    @pl.when(both(kind_a, height < 3))
    def _():
        greet_chips(parent)

    @pl.when(a_even)
    def _():
        greet_chips(p + 4)

    @pl.when(top)
    def _():
        greet_chips(p + 8)

    pl.semaphore_wait(
        barrier,
        15 + jnp.where(y >= 2, 3, 0) + jnp.where(kind_a, jnp.where(lax.rem(x, 2) == 0, 8, 4), 0),
    )

    lend(C0, 1, fac, fac_sem, fac_sent)
    remote(force.at[pl.ds(2 * other, 2), 0], even_f.at[k], even_sent, even_sem, p, 2 * z + other)
    def pick(n, values):
        found = values[-1]
        for at in range(len(values) - 1):
            found = jnp.where(n == at, values[at], found)
        return found

    def send_odd(n, _):
        core, piece = pick(n, PIECE_CORE), pick(n, PIECE_OF_CORE)
        g, h = lax.div(piece, 2), lax.rem(piece, 2)
        src = force.at[2 * core + g, 1, :, pl.ds(pl.multiple_of(h * half, half), half)]
        for step in (2, 1, 3):
            remote(src, odd_v.at[g, h, c], odd_sent, odd_sem.at[g, h], p, 2 * ring(step) + core)

        @pl.when(core != k)
        def _():
            remote(src, odd_v.at[g, h, c], odd_sent, odd_sem.at[g, h], p, 2 * z + core)

        return 0

    def allowed(piece):
        come = jnp.where(
            k == 0, pick(piece, [n for n in range(8) if PIECE_CORE[n] == 0]),
            pick(piece, [n for n in range(8) if PIECE_CORE[n] == 1]),
        )
        return jnp.minimum(come + 1 + AHEAD, 8)

    lax.fori_loop(0, AHEAD, send_odd, 0)

    def spread_factor(which, n=0, of=1):
        size = coupling.shape[4] // of
        at = pl.ds(pl.multiple_of(n * size, size), size)
        for core in range(2):
            remote(
                factor(which, 0, 2 * core + 1).at[:, at], upp.at[which, k, :, at], upp_sent, upp_sem.at[which],
                4 * x + lax.rem(y + 1 + 2 * core, 4), 2 * z + core,
            )

    pl.when(p == 0)(lambda: spread_factor(INV))
    pl.when(both(even, p > 0))(lambda: spread_factor(C0))

    for which in (C0, INV, C1):
        @pl.when(odd)
        def _():
            lend(which, 0, mid, mid_sem, mid_sent)

        @pl.when(even if which == INV else both(even, p > 0))
        def _():
            remote(
                factor(which, 0, 2 * other), upp.at[which, k], upp_lent, upp_sem.at[which],
                p, 2 * z + other,
            )

        if which != C0:
            lend(which, 1, fac, fac_sem, fac_sent)

    def times(panel, ref):
        wide = jnp.concatenate([ref[0, 0], ref[1, 0], ref[0, 1], ref[1, 1]], axis=1)
        product = jnp.dot(panel, wide, preferred_element_type=F32)
        n = wide.shape[1] // 2
        real = product[:cut, :n] + product[cut:, n:]
        imag = product[cut:, :n] - product[:cut, n:]
        return jnp.concatenate([real, imag], axis=0)

    def across(ref, i):
        return jnp.concatenate([ref[i, chip] for chip in range(CHIPS)], axis=1)

    def place(i):
        g = lax.div(i, CUTS)
        q = lax.rem(i, CUTS)
        h = lax.div(q, CUTS // 2)
        r = lax.rem(q, CUTS // 2)
        return g, q, h, pl.multiple_of(r * cut, cut)

    def rows_of(q):
        return pl.ds(pl.multiple_of(q * cut, cut), cut)

    def odd_panel(i):
        g, _, h, r = place(i)
        parts = [
            jnp.concatenate([odd_v[g, h, col, part, pl.ds(r, cut)] for col in range(2 * CHIPS)], axis=1)
            for part in range(2)
        ]
        return jnp.concatenate(parts, axis=0)

    def along(ref, i, sent, sem):
        for step in (1, 3, 2):
            remote(ref.at[i, z], ref.at[i, z], sent, sem.at[i], p, 2 * ring(step) + k)

    def straight(src, dst, sent, got, column):
        for step in (2, 1, 3, 0):
            remote(src, dst, sent, got, column, 2 * ring(step) + k)

    def write_out(i, row, value):
        g, q, _, _ = place(i)
        at = rows_of(q)
        for side in range(2):
            for part in range(2):
                stage[side, g, row, part, at] = value[part * cut:(part + 1) * cut, side * 128:(side + 1) * 128]
        if row:
            local(stage.at[k, g, row, :, at], out.at[2 * k + g, row, :, at], out_kept)
            remote(
                stage.at[other, g, row, :, at], out.at[2 * k + g, row, :, at], out_sent, out_sem,
                p, 2 * z + other,
            )
            return

        @pl.when(q == CUTS - 1)
        def _():
            local(stage.at[k, g, row], out.at[2 * k + g, row], out_kept)
            remote(
                stage.at[other, g, row], out.at[2 * k + g, row], out_sent, out_sem, p, 2 * z + other
            )

    def write_upper(j, value):
        at = rows_of(j)
        freq = 2 * k + up_g
        for side in range(2):
            for part in range(2):
                up_stage[side, part, at] = value[part * cut:(part + 1) * cut, side * 128:(side + 1) * 128]

        @pl.when(both(even, j == CUTS - 1))
        def _():
            local(up_stage.at[k], out.at[freq, 0], up_stage_kept)
            remote(up_stage.at[other], out.at[freq, 0], up_stage_sent, out_core_sem, p, 2 * z + other)

        @pl.when(both(odd, j == CUTS - 1))
        def _():
            for side in range(2):
                remote(
                    up_stage.at[side], out.at[freq, 0], up_stage_sent, out_far_sem, home, 2 * z + side
                )

    def await_factor(ref, which, sem):
        for g in range(2):
            await_bytes(ref.at[which, g], sem.at[which, g])

    def await_upper(which):
        await_bytes(upp.at[which], upp_sem.at[which])

    def once(i, work):
        pl.when(i == 0)(work)

    def reduce_odd(i):
        g, q, h, _ = place(i)

        @pl.when(lax.rem(q, CUTS // 2) == 0)
        def _():
            await_bytes(odd_v.at[g, h], odd_sem.at[g, h])
            piece = 2 * g + h
            sent = jnp.where(piece == 0, AHEAD, allowed(piece - 1))
            lax.fori_loop(sent, jnp.where(piece == 3, 8, allowed(piece)), send_odd, 0)

        at = rows_of(q)
        mine = jnp.concatenate(
            [
                jnp.concatenate([even_f[side, g, part, at] for side in range(2)], axis=1)
                for part in range(2)
            ],
            axis=0,
        )
        left = (mine.astype(F32) - times(odd_panel(i), fac.at[C0, g])).astype(BF16)

        @pl.when(odd)
        def _():
            base[i, z] = left
            along(base, i, base_sent, base_sem)

        @pl.when(both(even, g == 0))
        def _():
            up_base[q] = left

        @pl.when(both(even, g == 1))
        def _():
            shard[q] = left
            remote(shard.at[q], up_base.at[q], shard_sent, up_base_sem.at[q], beside, c)

    def reduce_middle(i):
        g, q, _, _ = place(i)
        once(i, lambda: await_factor(mid, C0, mid_sem))
        await_bytes(base.at[i, pl.ds(0, 3)], base_sem.at[i])
        mid_out[i] = times(across(base, i), mid.at[C0, g]).astype(BF16)

        @pl.when(g == 0)
        def _():
            remote(mid_out.at[i], up_mid.at[q], mid_out_sent, up_mid_sem.at[q], p - 1, c)

        @pl.when(both(g == 1, k == 0))
        def _():
            local(mid_out.at[i], up_mid.at[q], up_mid_sem.at[q])

        @pl.when(both(g == 1, k == 1))
        def _():
            remote(mid_out.at[i], up_mid.at[q], mid_out_sent, up_mid_sem.at[q], twin, c)

    def inverse_odd(i):
        g, _, _, _ = place(i)
        once(i, lambda: await_factor(fac, INV, fac_sem))
        inv_odd[i] = times(odd_panel(i), fac.at[INV, g])

    def inverse_middle(i):
        g, _, _, _ = place(i)
        once(i, lambda: await_factor(mid, INV, mid_sem))
        inv_even[i] = times(across(base, i), mid.at[INV, g])

    def settle_upper(j):
        @pl.when(odd)
        def _():
            await_bytes(up_base.at[j], up_base_sem.at[j])

        await_bytes(up_mid.at[j], up_mid_sem.at[j])
        up_all[j, z] = (up_base[j].astype(F32) - up_mid[j].astype(F32)).astype(BF16)
        along(up_all, j, up_all_sent, up_all_sem)

    def reduce_upper(j):
        once(j, lambda: pl.when(inner)(lambda: await_upper(C0)))
        once(j, lambda: pl.when(top)(lambda: await_upper(INV)))
        await_bytes(up_all.at[j, pl.ds(0, 3)], up_all_sem.at[j])

        @pl.when(height == 0)
        def _():
            up_red[j] = up_all[j]

        for level in range(3):
            @pl.when(level < height)
            def _():
                await_bytes(up_upd.at[level, j], up_upd_sem.at[level, j])
                before = up_all[j].astype(F32) if level == 0 else acc[...]
                acc[...] = before - up_upd[level, j].astype(F32)

        @pl.when(height > 0)
        def _():
            up_red[j] = acc[...].astype(BF16)

        product = times(across(up_red, j), upp.at[jnp.where(top, INV, C0)])

        @pl.when(inner)
        def _():
            up_out[j] = product.astype(BF16)
            straight(up_out.at[j], up_upd.at[height, j, z], up_out_sent, up_upd_sem.at[height, j], parent)

        @pl.when(top)
        def _():
            solved_upper(j, product)

    def inverse_upper(j):
        once(j, lambda: await_upper(INV))
        up_inv[j] = times(across(up_red, j), upp.at[INV])

    def solved_upper(j, value):
        i = up_g * CUTS + j
        panel = value.astype(BF16)
        up_own[j] = panel

        @pl.when(height > 0)
        def _():
            straight(up_own.at[j], up_low.at[j, z], up_first_sent, up_low_sem.at[j], first)

        @pl.when(both(kind_b, jnp.logical_not(child_here)))
        def _():
            straight(up_own.at[j], low.at[i, z], up_first_sent, low_sem.at[i], child)

        @pl.when(child_here)
        def _():
            low[i, z] = panel
            along(low, i, low_sent, low_sem)

        @pl.when(top)
        def _():
            remote(up_own.at[j], up_low.at[j, z], shard_out_sent.at[0], up_shard_sem.at[j], p + 4, c)

        @pl.when(a_even)
        def _():
            remote(up_own.at[j], up_low.at[j, z], shard_out_sent.at[1], up_shard_sem.at[j], twin, c)

        @pl.when(both(kind_a, jnp.logical_not(child_here)))
        def _():
            remote(up_own.at[j], low.at[i, z], shard_out_sent.at[2], low_shard_sem.at[i], child, c)

        @pl.when(odd)
        def _():
            remote(up_own.at[j], own.at[i, z], shard_out_sent.at[3], own_shard_sem.at[j], home, c)

        @pl.when(even)
        def _():
            own[i, z] = panel
            along(own, i, own_sent, own_sem)

        write_upper(j, value)

    def spread_upper(j):
        await_bytes(up_low.at[j, 0], up_shard_sem.at[j])
        along(up_low, j, up_low_sent, up_low_sem)

    def spread_low(i):
        @pl.when(jnp.logical_not(both(child_here, i >= CUTS)))
        def _():
            await_bytes(low.at[i, 0], low_shard_sem.at[i])
            along(low, i, low_sent, low_sem)

    def spread_own(j):
        await_bytes(own.at[CUTS + j, 0], own_shard_sem.at[j])
        along(own, CUTS + j, own_sent, own_sem)

    def back_upper(j):
        once(j, lambda: await_upper(C1))

        @pl.when(by_shard)
        def _():
            await_bytes(up_low.at[j, pl.ds(0, 3)], up_low_sem.at[j])

        @pl.when(jnp.logical_not(by_shard))
        def _():
            await_bytes(up_low.at[j], up_low_sem.at[j])

        solved_upper(j, up_inv[j] - times(across(up_low, j), upp.at[C1]))

    def back_middle(i):
        g, _, _, _ = place(i)
        once(i, lambda: await_factor(mid, C1, mid_sem))
        whole = both(y == 3, jnp.logical_not(both(child_here, g == 1)))

        @pl.when(whole)
        def _():
            await_bytes(low.at[i], low_sem.at[i])

        @pl.when(jnp.logical_not(whole))
        def _():
            await_bytes(low.at[i, pl.ds(0, 3)], low_sem.at[i])

        value = inv_even[i] - times(across(low, i), mid.at[C1, g])
        own[i, z] = value.astype(BF16)
        along(own, i, own_sent, own_sem)
        write_out(i, 0, value)

    def back_odd(i):
        g, _, _, _ = place(i)
        once(i, lambda: await_factor(fac, C1, fac_sem))

        await_bytes(own.at[i, pl.ds(0, 3)], own_sem.at[i])
        write_out(i, 1, inv_odd[i] - times(across(own, i), fac.at[C1, g]))

    at_settle = jnp.where(even, MIDDLE + 3, MIDDLE + 7)
    at_upper = at_settle + jnp.where(kind_b, SETTLE, CUTS)
    at_middle_inverse = MIDDLE + 7 + 2 * CUTS
    at_back = at_middle_inverse + chunks + CUTS
    at_end = at_back + SETTLE + 3

    for g in range(2):
        await_bytes(fac.at[C0, g], fac_sem.at[C0, g])
    await_bytes(even_f, even_sem)

    def step(s, _):
        def during(start, count, work, who=None):
            i = s - start
            now = both(i >= 0, i < count)

            @pl.when(now if who is None else both(now, who))
            def _():
                work(i)

        during(0, chunks, reduce_odd)
        at_move = jnp.where(kind_a, CUTS, MIDDLE + 3 + SETTLE + CUTS)
        during(at_move, PIECES, lambda n: spread_factor(INV, n, PIECES), both(even, p > 0))
        during(at_move + jnp.where(kind_a, 2, PIECES), PIECES, lambda n: spread_factor(C1, n, PIECES), both(even, p > 0))
        during(MIDDLE, chunks, reduce_middle, odd)
        during(MIDDLE + 1, chunks, inverse_odd)
        during(at_settle, CUTS, settle_upper)
        during(at_upper, CUTS, reduce_upper)
        during(jnp.where(even, at_upper, at_back - CUTS), CUTS, inverse_upper, inner)
        during(at_middle_inverse, chunks, inverse_middle, odd)
        during(at_back, CUTS, spread_upper, by_shard)
        during(at_back + SETTLE, CUTS, back_upper, inner)
        during(at_back, chunks, spread_low, y == 1)
        during(at_back + SETTLE, chunks, back_middle, odd)
        during(at_back + SETTLE + CUTS, CUTS, spread_own, even)
        during(at_end, chunks, back_odd)
        return 0

    lax.fori_loop(0, at_end + chunks, step, 0)

    await_bytes(fac.at[:, 0], fac_sent)
    await_bytes(odd_v.at[:, :, pl.ds(0, 7)], odd_sent)
    await_bytes(even_f.at[0], even_sent)
    await_bytes(up_all.at[:, pl.ds(0, 3)], up_all_sent)
    await_bytes(own.at[:, pl.ds(0, 3)], own_sent)

    @pl.when(inner)
    def _():
        await_bytes(up_all, up_out_sent)

    @pl.when(jnp.logical_not(both(kind_b, child_here)))
    def _():
        await_bytes(up_all, up_first_sent)

    @pl.when(top)
    def _():
        await_bytes(up_own, shard_out_sent.at[0])

    @pl.when(a_even)
    def _():
        await_bytes(up_own, shard_out_sent.at[1])

    @pl.when(both(kind_a, jnp.logical_not(child_here)))
    def _():
        await_bytes(up_own, shard_out_sent.at[2])

    @pl.when(odd)
    def _():
        await_bytes(mid.at[:, 0], mid_sent)
        await_bytes(base.at[:, pl.ds(0, 3)], base_sent)
        await_bytes(up_own, shard_out_sent.at[3])
        await_bytes(stage.at[0], out_kept)
        await_bytes(stage.at[0], out_sent)
        await_bytes(stage.at[0], out_sem)
        await_bytes(up_stage, up_stage_sent)

    @pl.when(by_shard)
    def _():
        await_bytes(up_low.at[:, pl.ds(0, 3)], up_low_sent)

    @pl.when(y == 1)
    def _():
        await_bytes(low.at[:, pl.ds(0, 3)], low_sent)

    @pl.when(both(y == 3, k == 0))
    def _():
        await_bytes(low.at[pl.ds(0, CUTS), pl.ds(0, 3)], low_sent)

    @pl.when(both(odd, k == 0))
    def _():
        await_bytes(mid_out.at[pl.ds(0, CUTS)], mid_out_sent)

    @pl.when(both(odd, k == 1))
    def _():
        await_bytes(mid_out, mid_out_sent)

    @pl.when(p == 0)
    def _():
        await_bytes(upp.at[INV], upp_sent)
        await_bytes(upp.at[INV, 0], upp_lent)

    @pl.when(both(even, p > 0))
    def _():
        await_bytes(upp, upp_sent)
        await_bytes(upp.at[:, 0], upp_lent)

    @pl.when(even)
    def _():
        await_bytes(shard, shard_sent)
        await_bytes(stage.at[0, 0], out_kept)
        await_bytes(stage.at[0, 0], out_sent)
        await_bytes(stage.at[0, 0], out_sem)
        await_bytes(up_stage.at[0], up_stage_kept)
        await_bytes(up_stage.at[0], up_stage_sent)
        await_bytes(up_stage.at[0], out_core_sem)
        await_bytes(up_stage, out_far_sem)


def local_solve(force, inverse, coupling):
    rhs, cols = force.shape[3:]
    block = inverse.shape[3]
    chunks = 2 * CUTS
    rows = 2 * rhs // CUTS
    wide = 2 * cols
    dma = pltpu.SemaphoreType.DMA
    piece = (rows, wide)
    panel = (chunks, CHIPS) + piece
    upper = (CUTS, CHIPS) + piece
    weight = (2, 2, block, cols)
    hbm = pl.BlockSpec(memory_space=pl.ANY)
    return pl.pallas_call(
        kernel,
        out_shape=jax.ShapeDtypeStruct(force.shape, F32),
        in_specs=[hbm] * 3,
        out_specs=hbm,
        scratch_shapes=[
            pltpu.VMEM((3, 2) + weight, BF16),
            pltpu.VMEM((3, 2) + weight, BF16),
            pltpu.VMEM((3,) + weight, BF16),
            pltpu.VMEM((2, 2, 2 * CHIPS, 2, rhs // 2, cols), BF16),
            pltpu.VMEM((2, 2, 2, rhs, cols), BF16),
            pltpu.VMEM(panel, BF16),
            pltpu.VMEM((CUTS,) + piece, BF16),
            pltpu.VMEM((chunks,) + piece, BF16),
            pltpu.VMEM((CUTS,) + piece, BF16),
            pltpu.VMEM((CUTS,) + piece, BF16),
            pltpu.VMEM(upper, BF16),
            pltpu.VMEM((3,) + upper, BF16),
            pltpu.VMEM((CUTS,) + piece, BF16),
            pltpu.VMEM(upper, BF16),
            pltpu.VMEM((CUTS,) + piece, F32),
            pltpu.VMEM(upper, BF16),
            pltpu.VMEM((CUTS,) + piece, BF16),
            pltpu.VMEM((chunks,) + piece, F32),
            pltpu.VMEM((chunks,) + piece, F32),
            pltpu.VMEM(panel, BF16),
            pltpu.VMEM(panel, BF16),
            pltpu.VMEM((2, 2, 2, 2, rhs, cols), F32),
            pltpu.VMEM((2, 2, rhs, cols), F32),
            pltpu.VMEM((CHIPS,) + piece, F32),
            dma((3, 2)), dma((3, 2)), dma((3,)), dma((2, 2)), dma, dma((chunks,)), dma((CUTS,)), dma((CUTS,)),
            dma((CUTS,)), dma((3, CUTS)), dma((CUTS,)), dma((chunks,)), dma((chunks,)), dma((CUTS,)),
            dma((chunks,)), dma((CUTS,)), dma, dma, dma,
            dma, dma, dma, dma, dma, dma, dma, dma, dma, dma, dma, dma, dma((4,)), dma, dma, dma, dma, dma, dma, dma,
        ],
        compiler_params=pltpu.CompilerParams(
            collective_id=0, has_side_effects=True, vmem_limit_bytes=60 * 2**20
        ),
        name="resolvent",
    )(force, inverse, coupling)


def solution(mesh):
    return jax.shard_map(
        local_solve,
        mesh=mesh,
        in_specs=(
            P(None, "radial", None, None, "col"),
            P(None, "radial", None, None, "col"),
            P(None, "radial", None, None, None, "col"),
        ),
        out_specs=P(None, "radial", None, None, "col"),
        check_vma=False,
    )
```
